32 devices in a mesh: rows: 8 (over y, x, core), cols: 4 (over z).
Axes of the slice: x: 2, y: 2, z: 4, core: 2. Of those that a mesh axis runs over, the one named last changes fastest.
Arguments:
- sources: float32 [8, 384, 1536], P(None, 'rows', 'cols'), may hold values from -6 to 6
- sample_maps: float32 [8, 384, 1536], P(None, 'rows', 'cols'), may hold values from 0 to 1
- conductance: float32 [384, 1536], P('rows', 'cols'), may hold values from 0.2 to 5
- shunt: float32 [384, 1536], P('rows', 'cols'), may hold values from 0.001 to 0.01
- nodata_mask: int32 [384, 1536], P('rows', 'cols'), may hold values 0 or 1
- deme_cells: int32 [8], replicated, may hold values from 0 to 589823
- pair_weights: float32 [8, 8], replicated, may hold values from -6 to 6
Outputs:
- solution: float32 [16, 384, 1536], P(None, 'rows', 'cols')
- conductance_grad: float32 [384, 1536], P('rows', 'cols')
The draws below stay inside these ranges and needn't reach their ends.
All inputs are finite; a program needn't handle non-finite values. No bound on the sum of `nodata_mask` on one device may be relied on, other than what follows from the above.
Results may differ from the reference program's by a relative error of at most 0.0003.
Values sent between devices are 32-bit elements; how exact they have to be, the bound alone decides.
No kernel may reach another device: no remote copies, remote signals or barrier semaphores. Data moves between devices by JAX's collectives and lax.ppermute only.
A program may use at most 64 MiB of HBM per device.

```python
import math
import jax
import jax.numpy as jnp
from jax import lax

DEMES = 8
ITERS = 5
NR = 384
NC = 1536


def set_ends(result, key, smallest, largest):
    longest = result.shape.index(max(result.shape))
    spots = []
    for shift in (0, 1):
        where = [jax.random.randint(jax.random.fold_in(key, axis), (), 0, length) for axis, length in enumerate(result.shape)]
        where[longest] = (where[longest] + shift) % result.shape[longest]
        spots.append(tuple(where))
    return result.at[spots[0]].set(smallest).at[spots[1]].set(largest)


def block_scale(rng, extent, pieces, least, largest):
    loudness = 1.0
    for dim, shards_of in pieces:
        heights = jax.random.uniform(jax.random.fold_in(jax.random.fold_in(rng, 6), dim), (shards_of,), jnp.float32, least / len(pieces), largest / len(pieces))
        loudness = loudness * jnp.repeat(jnp.exp(heights), extent[dim] // shards_of).reshape((-1,) + (1,) * (len(extent) - 1 - dim))
    return loudness


def noise(key, extent, deviation, limit, shards=(), kind=jnp.bfloat16):
    factor_of = block_scale(key, extent, shards, -0.22, 0.18) if shards else 1.0
    array = jax.random.normal(key, extent, jnp.float32) * deviation * factor_of
    return jnp.minimum(jnp.maximum(array, -limit), limit).astype(kind)


def setup_inputs(seed: int = 0) -> dict:
    keys = jax.random.split(jax.random.key(seed), 8)
    return {
        "sources": noise(keys[0], (DEMES, NR, NC), 1.0, 6.0, ((1, 8), (2, 4)), jnp.float32),
        "sample_maps": jnp.clip(1.0 * jax.random.uniform(keys[1], (DEMES, NR, NC), jnp.float32) ** block_scale(keys[1], (DEMES, NR, NC), ((1, 8), (2, 4)), -0.2, 0.2), 0.0, 1.0),
        "conductance": jnp.clip(jnp.exp(math.log(5.0) - 3.218876 * jax.random.uniform(keys[2], (NR, NC), jnp.float32) ** block_scale(keys[2], (NR, NC), ((0, 8), (1, 4)), -0.2, 0.2)), 0.2, 5.0),
        "shunt": jnp.clip(jnp.exp(math.log(0.01) - 2.30258502 * jax.random.uniform(keys[3], (NR, NC), jnp.float32) ** block_scale(keys[3], (NR, NC), ((0, 8), (1, 4)), -0.2, 0.2)), 0.001, 0.01),
        "nodata_mask": set_ends((jax.random.randint(keys[4], (NR, NC), 0, 10) < 9).astype(jnp.int32), jax.random.fold_in(keys[4], 1), 0, 1),
        "deme_cells": set_ends(jax.random.randint(keys[5], (DEMES,), 0, NR * NC), jax.random.fold_in(keys[5], 1), 0, (NR * NC) - 1).astype(jnp.int32),
        "pair_weights": noise(keys[6], (DEMES, DEMES), 1.0, 6.0, (), jnp.float32),
    }


def edge_weights(scaled, masked):
    padded_scaled = jnp.pad(scaled, 1)
    padded_mask = jnp.pad(masked, 1)
    row_count, col_count = scaled.shape
    weights = []
    half_links = []
    for row_start, col_start in ((2, 1), (0, 1), (1, 2), (1, 0)):
        other = padded_scaled[row_start:row_start + row_count, col_start:col_start + col_count]
        other_mask = padded_mask[row_start:row_start + row_count, col_start:col_start + col_count]
        pair = masked * other_mask
        weights.append(0.5 * (scaled + other) * pair)
        half_links.append(0.5 * pair)
    return weights, half_links


def operate(fields, weights, diagonal):
    padded = jnp.pad(fields, ((0, 0), (1, 1), (1, 1)))
    to_south = weights[0] * padded[:, 2:, 1:-1]
    to_north = weights[1] * padded[:, :-2, 1:-1]
    to_east = weights[2] * padded[:, 1:-1, 2:]
    to_west = weights[3] * padded[:, 1:-1, :-2]
    return diagonal * fields - (to_south + to_north + to_east + to_west)


def reduce_pairs(first, second):
    return jnp.sum(first * second, axis=(1, 2))


def link_product(fields, others, link, deme_count):
    differ = fields - others
    return link * jnp.sum(differ[:deme_count] * differ[deme_count:], axis=0)


def reference(sources, sample_maps, conductance, shunt, nodata_mask, deme_cells, pair_weights):
    deme_count = sources.shape[0]
    row_count, col_count = conductance.shape
    masked = nodata_mask.astype(jnp.float32)
    scaled = masked * conductance
    weights, half_links = edge_weights(scaled, masked)
    diagonal = shunt + weights[0] + weights[1] + weights[2] + weights[3]
    global_rows = jnp.arange(row_count, dtype=jnp.int32)
    global_cols = jnp.arange(col_count, dtype=jnp.int32)
    deme_rows = deme_cells // col_count
    deme_cols = deme_cells % col_count
    deme_hits = ((global_rows[None, :, None] == deme_rows[:, None, None])
                 & (global_cols[None, None, :] == deme_cols[:, None, None])).astype(jnp.float32)
    readout = sample_maps + 4.0 * deme_hits
    adjoint_rhs = jnp.einsum("kj,jrc->krc", pair_weights, readout, precision=lax.Precision.HIGHEST)
    right_sides = masked * jnp.concatenate([sources, adjoint_rhs], 0)
    solution = jnp.zeros_like(right_sides)
    residual = right_sides
    scaled_res = residual / diagonal
    direction = scaled_res
    norm_now = reduce_pairs(residual, scaled_res)
    for counter in range(ITERS):
        image = operate(direction, weights, diagonal)
        step_size = (norm_now / reduce_pairs(direction, image))[:, None, None]
        solution = solution + step_size * direction
        residual = residual - step_size * image
        scaled_res = residual / diagonal
        norm_next = reduce_pairs(residual, scaled_res)
        direction = scaled_res + (norm_next / norm_now)[:, None, None] * direction
        norm_now = norm_next
    padded = jnp.pad(solution, ((0, 0), (1, 1), (1, 1)))
    to_south = link_product(solution, padded[:, 2:, 1:-1], half_links[0], deme_count)
    to_north = link_product(solution, padded[:, :-2, 1:-1], half_links[1], deme_count)
    to_east = link_product(solution, padded[:, 1:-1, 2:], half_links[2], deme_count)
    to_west = link_product(solution, padded[:, 1:-1, :-2], half_links[3], deme_count)
    conductance_grad = -(to_south + to_north + to_east + to_west)
    return solution, conductance_grad
```

```python
import functools

import jax
import jax.numpy as jnp
from jax import lax
from jax.experimental import pallas as pl
from jax.experimental.pallas import tpu as pltpu
from jax.sharding import PartitionSpec as P

ITERS = 5
LANES = 128
SUBS = 8
VMEM = pl.BlockSpec(memory_space=pltpu.VMEM)
SMEM = pl.BlockSpec(memory_space=pltpu.SMEM)
LIMIT = 40 * 1024 * 1024


def swaps(count, first):
    pairs = [(i, i + 1) for i in range(first, count - 1, 2)]
    return pairs + [(b, a) for a, b in pairs]


def lane_iota():
    return lax.broadcasted_iota(jnp.int32, (SUBS, LANES), 1)


def scaled_of(conductance, mask):
    return jnp.where(mask != 0, conductance, 0.0)


def pack_rows(src, maps, cond, shunt, mask, a_out, b_out):
    even = lax.rem(lax.axis_index("rows"), 2) == 0
    rows = cond.shape[0]
    demes = src.shape[0]
    scaled_n = scaled_of(cond[0 : ITERS + 1, :], mask[0 : ITERS + 1, :])
    scaled_s = scaled_of(cond[rows - ITERS - 1 : rows, :], mask[rows - ITERS - 1 : rows, :])
    pieces = [(src[f, 0:ITERS, :], src[f, rows - ITERS : rows, :]) for f in range(demes)]
    pieces += [(maps[f, 0:ITERS, :], maps[f, rows - ITERS : rows, :]) for f in range(demes)]
    pieces += [(shunt[0:ITERS, :], shunt[rows - ITERS : rows, :]), (scaled_n, scaled_s)]
    at = 0
    for north, south in pieces:
        size = north.shape[0]
        a_out[at : at + size, :] = jnp.where(even, south, north)
        b_out[at : at + size, :] = jnp.where(even, north, south)
        at += size


def halo_rows(even, got_a, got_b, at, size, lo, hi):
    a = got_a[at : at + size, lo:hi]
    b = got_b[at : at + size, lo:hi]
    return jnp.where(even, b, a), jnp.where(even, a, b)


def pack_cols(src, maps, cond, shunt, mask, got_a, got_b, c_out, d_out, edge):
    row_even = lax.rem(lax.axis_index("rows"), 2) == 0
    col_even = lax.rem(lax.axis_index("cols"), 2) == 0
    rows, cols = cond.shape
    demes = src.shape[0]
    planes = 2 * demes + 2
    tiles = rows // SUBS + 2
    last = cols - LANES
    edge[...] = jnp.zeros_like(edge)
    for f in range(planes):
        size = ITERS + (f == planes - 1)
        for side, lo in enumerate((0, last)):
            north, south = halo_rows(row_even, got_a, got_b, f * ITERS, size, lo, lo + LANES)
            edge[side, f, SUBS - size : SUBS, :] = north
            edge[side, f, SUBS : SUBS + size, :] = south
    lane = lane_iota()
    for k in range(tiles):
        both = []
        for side, lo in enumerate((0, last)):
            total = jnp.zeros((SUBS, LANES), jnp.float32)
            for f in range(planes):
                size = ITERS + (f == planes - 1)
                if k == 0:
                    piece = edge[side, f, 0:SUBS, :]
                elif k == tiles - 1:
                    piece = edge[side, f, SUBS : 2 * SUBS, :]
                else:
                    r = slice((k - 1) * SUBS, k * SUBS)
                    c = slice(lo, lo + LANES)
                    if f < demes:
                        piece = src[f, r, c]
                    elif f < 2 * demes:
                        piece = maps[f - demes, r, c]
                    elif f == 2 * demes:
                        piece = shunt[r, c]
                    else:
                        piece = scaled_of(cond[r, c], mask[r, c])
                start = 0 if side == 0 else LANES - size
                shift = (f * ITERS - start) % LANES
                moved = pltpu.roll(piece, shift, 1) if shift else piece
                keep = (lane >= f * ITERS) & (lane < f * ITERS + size)
                total = jnp.where(keep, moved, total)
            both.append(total)
        west, east = both
        r = slice(k * SUBS, (k + 1) * SUBS)
        c_out[r, :] = jnp.where(col_even, east, west)
        d_out[r, :] = jnp.where(col_even, west, east)


def two_sum(a, b):
    s = a + b
    t = s - a
    return s, (a - (s - t)) + (b - t)


def quick(a, b):
    s = a + b
    return s, b - (s - a)


def split(a):
    c = 4097.0 * a
    high = c - (c - a)
    return high, a - high


def two_prod(a, b):
    p = a * b
    ah, al = split(a)
    bh, bl = split(b)
    return p, ((ah * bh - p) + ah * bl + al * bh) + al * bl


def dadd(x, y):
    s, e = two_sum(x[0], y[0])
    return quick(s, e + (x[1] + y[1]))


def dneg(x):
    return -x[0], -x[1]


def dsub(x, y):
    return dadd(x, dneg(y))


def dmul(x, y):
    p, e = two_prod(x[0], y[0])
    return quick(p, e + (x[0] * y[1] + x[1] * y[0]))


def dscale(x, power_of_two):
    return x[0] * power_of_two, x[1] * power_of_two


def ddiv(x, y):
    q = x[0] / y[0]
    p, e = two_prod(q, y[0])
    rest = (x[0] - p) - e + x[1] - q * y[1]
    return quick(q, rest / y[0])


def dclamp(x, low, high):
    h = jnp.where(x[0] < low, low, jnp.where(x[0] > high, high, x[0]))
    return h, jnp.where(h == x[0], x[1], 0.0)


def polynomial(mu):
    zero = (jnp.zeros_like(mu[0][0]), jnp.zeros_like(mu[0][0]))
    one = (jnp.ones_like(mu[0][0]), zero[0])
    before, now = None, {l: mu[l] for l in range(2 * ITERS)}
    alphas, betas = [], [None]
    ratio_before, norm_before = None, None
    for k in range(ITERS):
        norm = (jnp.maximum(now[k][0], 1e-30), jnp.where(now[k][0] > 1e-30, now[k][1], 0.0))
        ratio = ddiv(now[k + 1], norm)
        if k:
            ratio = dscale(ratio, 0.5)
            beta = ddiv(norm, norm_before)
            if k > 1:
                beta = dscale(beta, 0.5)
            betas.append(dclamp(beta, 0.0, 1.0))
        alpha = ratio if k == 0 else dsub(ratio, ratio_before)
        alphas.append(dclamp(alpha, -1.0, 1.0))
        ratio_before, norm_before = ratio, norm
        if k == ITERS - 1:
            break
        following = {}
        for l in range(k + 1, 2 * ITERS - 1 - k):
            value = dadd(now[l + 1], now[l - 1]) if l - 1 >= k else now[l + 1]
            value = dsub(dscale(value, 0.5), dmul(alphas[k], now[l]))
            if k:
                value = dsub(value, dmul(betas[k], before[l]))
            following[l] = value
        before, now = now, following
    pivots, gains = [], []
    for k in range(ITERS):
        pivot = dsub(one, alphas[k])
        gain = one
        if k:
            pivot = dsub(pivot, ddiv(betas[k], pivots[-1]))
            gain = ddiv(gains[-1], pivots[-1])
        pivots.append(dclamp(pivot, 1e-6, 4.0))
        gains.append(gain)
    y = [None] * ITERS
    for k in range(ITERS - 1, -1, -1):
        top = gains[k] if k == ITERS - 1 else dadd(gains[k], dmul(betas[k + 1], y[k + 1]))
        y[k] = ddiv(top, pivots[k])
    after, here = [], [y[ITERS - 1]]
    for k in range(ITERS - 2, -1, -1):
        out = [dneg(dmul(alphas[k], b)) for b in here] + [zero]
        out[0] = dadd(out[0], y[k])
        out[1] = dadd(out[1], here[0])
        for j in range(1, len(here)):
            half = dscale(here[j], 0.5)
            out[j + 1] = dadd(out[j + 1], half)
            out[j - 1] = dadd(out[j - 1], half)
        for j, b in enumerate(after):
            out[j] = dsub(out[j], dmul(betas[k + 1], b))
        after, here = here, out
    return [c[0] for c in here]


def shifted_rows(load, k, tiles, step):
    r = k * SUBS + step
    if r < 0 or r + SUBS > tiles * SUBS:
        return pltpu.roll(load(k * SUBS), (-step) % SUBS, 0)
    return load(r)


def shifted_lanes(centers, lane):
    count = len(centers)
    lower = [pltpu.roll(c, LANES - 1, 1) for c in centers]
    upper = [pltpu.roll(c, 1, 1) for c in centers]
    east = [jnp.where(lane == LANES - 1, lower[(t + 1) % count], lower[t]) for t in range(count)]
    west = [jnp.where(lane == 0, upper[t - 1], upper[t]) for t in range(count)]
    return east, west


def build_basis(
    src, maps, cond, shunt, mask, cells, pairs, got_a, got_b, got_c, got_d,
    basis, scaled, message, links, diag, inverse, leak, sums,
):
    row_even = lax.rem(lax.axis_index("rows"), 2) == 0
    col_even = lax.rem(lax.axis_index("cols"), 2) == 0
    rows, cols = cond.shape
    demes = src.shape[0]
    fields = 2 * demes
    spans = cols // LANES + 1
    tiles = rows // SUBS + 2
    lane = lane_iota()
    zero = jnp.zeros((SUBS, LANES), jnp.float32)

    def plane(f):
        if f < fields:
            return lambda t, r, v: basis.__setitem__((0, f, t, r, slice(None)), v)
        target = leak if f == fields else scaled
        return lambda t, r, v: target.__setitem__((t, r, slice(None)), v)

    for f in range(fields + 2):
        store = plane(f)
        size = ITERS + (f == fields + 1)
        for t in range(spans - 1):
            c = slice(t * LANES, (t + 1) * LANES)
            if f < demes:
                own = src[f, :, c]
            elif f < fields:
                own = maps[f - demes, :, c]
            elif f == fields:
                own = shunt[:, c]
            else:
                own = scaled_of(cond[:, c], mask[:, c])
            store(t, slice(SUBS, SUBS + rows), own)
            north, south = halo_rows(row_even, got_a, got_b, f * ITERS, size, t * LANES, (t + 1) * LANES)
            store(t, slice(0, SUBS), zero)
            store(t, slice(SUBS + rows, 2 * SUBS + rows), zero)
            store(t, slice(SUBS - size, SUBS), north)
            store(t, slice(SUBS + rows, SUBS + rows + size), south)
    for k in range(tiles):
        r = slice(k * SUBS, (k + 1) * SUBS)
        from_c, from_d = got_c[r, :], got_d[r, :]
        east = jnp.where(col_even, from_c, from_d)
        west = jnp.where(col_even, from_d, from_c)
        for f in range(fields + 2):
            size = ITERS + (f == fields + 1)
            first = pltpu.roll(east, (-f * ITERS) % LANES, 1) if f else east
            final = pltpu.roll(west, (LANES - size - f * ITERS) % LANES, 1)
            value = jnp.where(lane < size, first, jnp.where(lane >= LANES - size, final, 0.0))
            plane(f)(spans - 1, r, value)

    total_cols = cols * lax.axis_size("cols")
    for j in range(demes):
        cell = cells[j]
        row = lax.div(cell, total_cols) - lax.axis_index("rows") * rows
        col = lax.rem(cell, total_cols) - lax.axis_index("cols") * cols

        @pl.when((row >= -ITERS) & (row < rows + ITERS) & (col >= -ITERS) & (col < cols + ITERS))
        def _():
            spot = jnp.where(col < 0, col + spans * LANES, col)
            tile = lax.div(spot, LANES)
            at = spot - tile * LANES
            line = basis[0, demes + j, tile, pl.ds(row + SUBS, 1), :]
            here = lax.broadcasted_iota(jnp.int32, (1, LANES), 1) == at
            basis[0, demes + j, tile, pl.ds(row + SUBS, 1), :] = line + jnp.where(here, 4.0, 0.0)

    for k in range(tiles):
        r = slice(k * SUBS, (k + 1) * SUBS)
        centers = [scaled[t, r, :] for t in range(spans)]
        easts, wests = shifted_lanes(centers, lane)
        for t in range(spans):
            load = lambda at: scaled[t, at : at + SUBS, :]
            here = centers[t]
            others = [
                shifted_rows(load, k, tiles, 1), shifted_rows(load, k, tiles, -1), easts[t], wests[t],
            ]
            twice = [jnp.where(jnp.minimum(here, o) > 0.0, here + o, 0.0) for o in others]
            d = leak[t, r, :] + 0.5 * (twice[0] + twice[1] + twice[2] + twice[3])
            inv = jnp.where(d > 0.0, 1.0 / jnp.where(d > 0.0, d, 1.0), 0.0)
            for side in range(4):
                links[side, t, r, :] = twice[side] * inv
            diag[t, r, :] = d
            inverse[t, r, :] = jnp.where(here > 0.0, inv, 0.0)

    def finish(k, carry):
        r = pl.ds(pl.multiple_of(k * SUBS, SUBS), SUBS)
        for t in range(spans):
            inv = inverse[t, r, :]
            for f in range(demes):
                basis[0, f, t, r, :] = basis[0, f, t, r, :] * inv
            readout = [basis[0, demes + j, t, r, :] * inv for j in range(demes)]
            for f in range(demes):
                total = pairs[f, 0] * readout[0]
                for j in range(1, demes):
                    total = total + pairs[f, j] * readout[j]
                basis[0, demes + f, t, r, :] = total
        return carry

    lax.fori_loop(0, tiles, finish, 0)

    for step in range(ITERS):
        for k in range(tiles):
            own_rows = 0 < k < tiles - 1
            if step == ITERS - 1 and not own_rows:
                continue
            r = slice(k * SUBS, (k + 1) * SUBS)
            weights = [[links[side, t, r, :] for side in range(4)] for t in range(spans)]
            if step == 0:
                weights = [[0.5 * w for w in ws] for ws in weights]
            ds = [diag[t, r, :] for t in range(spans - 1)] if own_rows else None

            def field(f, carry, step=step, k=k, own_rows=own_rows, r=r, weights=weights, ds=ds):
                centers = [basis[step, f, t, r, :] for t in range(spans)]
                easts, wests = shifted_lanes(centers, lane)
                first = second = None
                for t in range(spans):
                    halo = t == spans - 1
                    if step == ITERS - 1 and halo:
                        continue
                    load = lambda at: basis[step, f, t, at : at + SUBS, :]
                    south = shifted_rows(load, k, tiles, 1)
                    north = shifted_rows(load, k, tiles, -1)
                    w = weights[t]
                    value = (w[0] * south + w[1] * north) + (w[2] * easts[t] + w[3] * wests[t])
                    if step:
                        value = value - basis[step - 1, f, t, r, :]
                    if step < ITERS - 1:
                        basis[step + 1, f, t, r, :] = value
                    if own_rows and not halo:
                        e = ds[t] * centers[t]
                        one, two = e * centers[t], e * value
                        first = one if first is None else first + one
                        second = two if second is None else second + two
                if own_rows:
                    if k == 1:
                        sums[2 * step, f] = first
                        sums[2 * step + 1, f] = second
                    else:
                        sums[2 * step, f] += first
                        sums[2 * step + 1, f] += second
                return carry

            lax.fori_loop(0, fields, field, 0, unroll=4)

    packed = zero
    for m in range(2 * ITERS):
        for half in range(2):
            value = jnp.sum(sums[m, half * demes : (half + 1) * demes], axis=1)
            high, low = value, zero
            shift = LANES // 2
            while shift:
                high, low = dadd((high, low), (pltpu.roll(high, shift, 1), pltpu.roll(low, shift, 1)))
                shift //= 2
            at = half * (LANES // 2) + m
            packed = jnp.where(lane == at, high, jnp.where(lane == at + 16, low, packed))
    message[...] = jnp.broadcast_to(packed[None], message.shape)


def combine(everyone, basis, scaled, solution, grad, potential):
    devices = everyone.shape[0]
    fields, rows, cols = solution.shape
    demes = fields // 2
    spans = cols // LANES + 1
    tiles = rows // SUBS + 2
    lane = lane_iota()
    zero = jnp.zeros((SUBS, LANES), jnp.float32)
    chains = [(everyone[i], zero) for i in range(4)]
    for i in range(4, devices):
        high, low = chains[i % 4]
        s, e = two_sum(high, everyone[i])
        chains[i % 4] = (s, low + e)
    total = dadd(dadd(*(quick(*c) for c in chains[:2])), dadd(*(quick(*c) for c in chains[2:])))
    total = dadd(total, tuple(pltpu.roll(part, LANES - 16, 1) for part in total))
    raw = [total] + [
        tuple(pltpu.roll(part, LANES - m, 1) for part in total) for m in range(1, 2 * ITERS)
    ]
    mu = raw[:2] + [dsub(dscale(raw[m], 2.0), raw[m % 2]) for m in range(2, 2 * ITERS)]
    coefficients = polynomial(mu)

    for f in range(fields):
        half, sub = divmod(f, demes)
        lo = half * (LANES // 2)
        c = [jnp.broadcast_to(v[sub : sub + 1, lo : lo + 1], (SUBS, LANES)) for v in coefficients]
        for k in range(tiles):
            r = slice(k * SUBS, (k + 1) * SUBS)
            own_rows = 0 < k < tiles - 1
            for t in range(spans if own_rows else spans - 1):
                value = c[0] * basis[0, f, t, r, :]
                for j in range(1, ITERS):
                    value = value + c[j] * basis[j, f, t, r, :]
                potential[f, t, r, :] = value
                if own_rows and t < spans - 1:
                    solution[f, (k - 1) * SUBS : k * SUBS, t * LANES : (t + 1) * LANES] = value

    def gradient(k, carry):
        base = pl.multiple_of(k * SUBS, SUBS)
        r = pl.ds(base, SUBS)
        totals = [[zero] * 4 for _ in range(spans - 1)]
        for f in range(demes):
            differ = []
            for g in (f, demes + f):
                centers = [potential[g, t, r, :] for t in range(spans)]
                easts, wests = shifted_lanes(centers, lane)
                differ.append(
                    [
                        (
                            centers[t] - potential[g, t, pl.ds(base + 1, SUBS), :],
                            centers[t] - potential[g, t, pl.ds(base - 1, SUBS), :],
                            centers[t] - easts[t],
                            centers[t] - wests[t],
                        )
                        for t in range(spans - 1)
                    ]
                )
            for t in range(spans - 1):
                for side in range(4):
                    totals[t][side] = totals[t][side] + differ[0][t][side] * differ[1][t][side]
        centers = [scaled[t, r, :] for t in range(spans)]
        easts, wests = shifted_lanes(centers, lane)
        for t in range(spans - 1):
            others = [
                scaled[t, pl.ds(base + 1, SUBS), :], scaled[t, pl.ds(base - 1, SUBS), :], easts[t], wests[t],
            ]
            value = zero
            for side in range(4):
                linked = jnp.minimum(centers[t], others[side]) > 0.0
                value = value + jnp.where(linked, totals[t][side], 0.0)
            grad[pl.ds(base - SUBS, SUBS), t * LANES : (t + 1) * LANES] = -0.5 * value
        return carry

    lax.fori_loop(1, tiles - 1, gradient, 0)


def on_device(sources, sample_maps, conductance, shunt, nodata_mask, deme_cells, pair_weights):
    demes, rows, cols = sources.shape
    fields = 2 * demes
    spans = cols // LANES + 1
    high = rows + 2 * SUBS
    slab = -(-((fields + 2) * ITERS + 1) // SUBS) * SUBS
    f32 = jnp.float32
    params = pltpu.CompilerParams(vmem_limit_bytes=LIMIT)
    block = (sources, sample_maps, conductance, shunt, nodata_mask)
    count_r, count_c = lax.axis_size("rows"), lax.axis_size("cols")

    send_a, send_b = pl.pallas_call(
        pack_rows,
        out_shape=[jax.ShapeDtypeStruct((slab, cols), f32)] * 2,
        in_specs=[VMEM] * 5,
        out_specs=[VMEM] * 2,
        compiler_params=params,
        name="pack_rows",
    )(*block)
    got_a = lax.ppermute(send_a, "rows", swaps(count_r, 0))
    got_b = lax.ppermute(send_b, "rows", swaps(count_r, 1))
    send_c, send_d = pl.pallas_call(
        pack_cols,
        out_shape=[jax.ShapeDtypeStruct((high, LANES), f32)] * 2,
        in_specs=[VMEM] * 7,
        out_specs=[VMEM] * 2,
        scratch_shapes=[pltpu.VMEM((2, fields + 2, 2 * SUBS, LANES), f32)],
        compiler_params=params,
        name="pack_cols",
    )(*block, got_a, got_b)
    got_c = lax.ppermute(send_c, "cols", swaps(count_c, 0))
    got_d = lax.ppermute(send_d, "cols", swaps(count_c, 1))

    everyone = count_r * count_c
    basis, scaled, message = pl.pallas_call(
        build_basis,
        out_shape=[
            pltpu.VMEM((ITERS, fields, spans, high, LANES), f32),
            pltpu.VMEM((spans, high, LANES), f32),
            jax.ShapeDtypeStruct((everyone, SUBS, LANES), f32),
        ],
        in_specs=[VMEM] * 5 + [SMEM] * 2 + [VMEM] * 4,
        out_specs=[VMEM] * 3,
        scratch_shapes=[
            pltpu.VMEM((4, spans, high, LANES), f32),
            pltpu.VMEM((spans, high, LANES), f32),
            pltpu.VMEM((spans, high, LANES), f32),
            pltpu.VMEM((spans, high, LANES), f32),
            pltpu.VMEM((2 * ITERS, fields, SUBS, LANES), f32),
        ],
        compiler_params=params,
        name="build_basis",
    )(*block, deme_cells, pair_weights, got_a, got_b, got_c, got_d)
    gathered = lax.all_to_all(message, ("rows", "cols"), 0, 0)
    return pl.pallas_call(
        combine,
        out_shape=[
            jax.ShapeDtypeStruct((fields, rows, cols), f32),
            jax.ShapeDtypeStruct((rows, cols), f32),
        ],
        in_specs=[VMEM] * 3,
        out_specs=[VMEM] * 2,
        scratch_shapes=[pltpu.VMEM((fields, spans, high, LANES), f32)],
        compiler_params=params,
        name="combine",
    )(gathered, basis, scaled)


def solution(mesh):
    return jax.shard_map(
        on_device,
        mesh=mesh,
        in_specs=(
            P(None, "rows", "cols"),
            P(None, "rows", "cols"),
            P("rows", "cols"),
            P("rows", "cols"),
            P("rows", "cols"),
            P(),
            P(),
        ),
        out_specs=(P(None, "rows", "cols"), P("rows", "cols")),
        check_vma=False,
    )
```

```python
import functools

import jax
import jax.numpy as jnp
from jax import lax
from jax.experimental import pallas as pl
from jax.experimental.pallas import tpu as pltpu
from jax.sharding import PartitionSpec as P

ITERS = 5
LANES = 128
SUBS = 8
VMEM = pl.BlockSpec(memory_space=pltpu.VMEM)
SMEM = pl.BlockSpec(memory_space=pltpu.SMEM)
LIMIT = 40 * 1024 * 1024


def swaps(count, first):
    pairs = [(i, i + 1) for i in range(first, count - 1, 2)]
    return pairs + [(b, a) for a, b in pairs]


def lane_iota():
    return lax.broadcasted_iota(jnp.int32, (SUBS, LANES), 1)


def scaled_of(conductance, mask):
    return jnp.where(mask != 0, conductance, 0.0)


def pack_rows(src, maps, cond, shunt, mask, a_out, b_out, raw, edges, flats, masks, sems):
    even = lax.rem(lax.axis_index("rows"), 2) == 0
    rows, cols = cond.shape
    demes = src.shape[0]
    fields = 2 * demes
    spans = cols // LANES
    flows = []

    def fetch(source, target):
        flow = pltpu.make_async_copy(source, target, sems.at[len(flows)])
        flow.start()
        flows.append(flow)

    for side, at in enumerate((0, rows - SUBS)):
        fetch(src.at[:, at : at + SUBS, :], edges.at[side, 0:demes])
        fetch(maps.at[:, at : at + SUBS, :], edges.at[side, demes:fields])
    fetch(shunt, flats.at[0])
    fetch(cond, flats.at[1])
    fetch(mask, masks)
    early = len(flows)
    for t in range(spans):
        c = slice(t * LANES, (t + 1) * LANES)
        fetch(src.at[:, :, c], raw.at[0:demes, t, SUBS : SUBS + rows, :])
        fetch(maps.at[:, :, c], raw.at[demes:fields, t, SUBS : SUBS + rows, :])
    for flow in flows[:early]:
        flow.wait()
    for t in range(spans):
        c = slice(t * LANES, (t + 1) * LANES)
        raw[fields, t, SUBS : SUBS + rows, :] = flats[0, :, c]
        raw[fields + 1, t, SUBS : SUBS + rows, :] = scaled_of(flats[1, :, c], masks[:, c])
    top, low = slice(0, ITERS), slice(rows - ITERS, rows)
    pieces = [(edges[0, f, 0:ITERS, :], edges[1, f, SUBS - ITERS : SUBS, :]) for f in range(fields)]
    pieces.append((flats[0, top, :], flats[0, low, :]))
    top, low = slice(0, ITERS + 1), slice(rows - ITERS - 1, rows)
    pieces.append(
        (scaled_of(flats[1, top, :], masks[top, :]), scaled_of(flats[1, low, :], masks[low, :]))
    )
    at = 0
    for north, south in pieces:
        size = north.shape[0]
        a_out[at : at + size, :] = jnp.where(even, south, north)
        b_out[at : at + size, :] = jnp.where(even, north, south)
        at += size
    for flow in flows[early:]:
        flow.wait()


def halo_rows(even, got_a, got_b, at, size, lo, hi):
    a = got_a[at : at + size, lo:hi]
    b = got_b[at : at + size, lo:hi]
    return jnp.where(even, b, a), jnp.where(even, a, b)


def pack_cols(raw, got_a, got_b, c_out, d_out, edge):
    row_even = lax.rem(lax.axis_index("rows"), 2) == 0
    col_even = lax.rem(lax.axis_index("cols"), 2) == 0
    planes, spans, high, _ = raw.shape
    tiles = high // SUBS
    cols = (spans - 1) * LANES
    last = cols - LANES
    edge[...] = jnp.zeros_like(edge)
    for f in range(planes):
        size = ITERS + (f == planes - 1)
        for side, lo in enumerate((0, last)):
            north, south = halo_rows(row_even, got_a, got_b, f * ITERS, size, lo, lo + LANES)
            edge[side, f, SUBS - size : SUBS, :] = north
            edge[side, f, SUBS : SUBS + size, :] = south
    lane = lane_iota()
    for k in range(tiles):
        both = []
        for side, lo in enumerate((0, last)):
            total = jnp.zeros((SUBS, LANES), jnp.float32)
            for f in range(planes):
                size = ITERS + (f == planes - 1)
                if k == 0:
                    piece = edge[side, f, 0:SUBS, :]
                elif k == tiles - 1:
                    piece = edge[side, f, SUBS : 2 * SUBS, :]
                else:
                    piece = raw[f, lo // LANES, k * SUBS : (k + 1) * SUBS, :]
                start = 0 if side == 0 else LANES - size
                shift = (f * ITERS - start) % LANES
                moved = pltpu.roll(piece, shift, 1) if shift else piece
                keep = (lane >= f * ITERS) & (lane < f * ITERS + size)
                total = jnp.where(keep, moved, total)
            both.append(total)
        west, east = both
        r = slice(k * SUBS, (k + 1) * SUBS)
        c_out[r, :] = jnp.where(col_even, east, west)
        d_out[r, :] = jnp.where(col_even, west, east)


def two_sum(a, b):
    s = a + b
    t = s - a
    return s, (a - (s - t)) + (b - t)


def quick(a, b):
    s = a + b
    return s, b - (s - a)


def split(a):
    c = 4097.0 * a
    high = c - (c - a)
    return high, a - high


def two_prod(a, b):
    p = a * b
    ah, al = split(a)
    bh, bl = split(b)
    return p, ((ah * bh - p) + ah * bl + al * bh) + al * bl


def dadd(x, y):
    s, e = two_sum(x[0], y[0])
    return quick(s, e + (x[1] + y[1]))


def dneg(x):
    return -x[0], -x[1]


def dsub(x, y):
    return dadd(x, dneg(y))


def dmul(x, y):
    p, e = two_prod(x[0], y[0])
    return quick(p, e + (x[0] * y[1] + x[1] * y[0]))


def dscale(x, power_of_two):
    return x[0] * power_of_two, x[1] * power_of_two


def ddiv(x, y):
    q = x[0] / y[0]
    p, e = two_prod(q, y[0])
    rest = (x[0] - p) - e + x[1] - q * y[1]
    return quick(q, rest / y[0])


def dclamp(x, low, high):
    h = jnp.where(x[0] < low, low, jnp.where(x[0] > high, high, x[0]))
    return h, jnp.where(h == x[0], x[1], 0.0)


def polynomial(mu):
    zero = (jnp.zeros_like(mu[0][0]), jnp.zeros_like(mu[0][0]))
    one = (jnp.ones_like(mu[0][0]), zero[0])
    before, now = None, {l: mu[l] for l in range(2 * ITERS)}
    alphas, betas = [], [None]
    ratio_before, norm_before = None, None
    for k in range(ITERS):
        norm = (jnp.maximum(now[k][0], 1e-30), jnp.where(now[k][0] > 1e-30, now[k][1], 0.0))
        ratio = ddiv(now[k + 1], norm)
        if k:
            ratio = dscale(ratio, 0.5)
            beta = ddiv(norm, norm_before)
            if k > 1:
                beta = dscale(beta, 0.5)
            betas.append(dclamp(beta, 0.0, 1.0))
        alpha = ratio if k == 0 else dsub(ratio, ratio_before)
        alphas.append(dclamp(alpha, -1.0, 1.0))
        ratio_before, norm_before = ratio, norm
        if k == ITERS - 1:
            break
        following = {}
        for l in range(k + 1, 2 * ITERS - 1 - k):
            value = dadd(now[l + 1], now[l - 1]) if l - 1 >= k else now[l + 1]
            value = dsub(dscale(value, 0.5), dmul(alphas[k], now[l]))
            if k:
                value = dsub(value, dmul(betas[k], before[l]))
            following[l] = value
        before, now = now, following
    pivots, gains = [], []
    for k in range(ITERS):
        pivot = dsub(one, alphas[k])
        gain = one
        if k:
            pivot = dsub(pivot, ddiv(betas[k], pivots[-1]))
            gain = ddiv(gains[-1], pivots[-1])
        pivots.append(dclamp(pivot, 1e-6, 4.0))
        gains.append(gain)
    y = [None] * ITERS
    for k in range(ITERS - 1, -1, -1):
        top = gains[k] if k == ITERS - 1 else dadd(gains[k], dmul(betas[k + 1], y[k + 1]))
        y[k] = ddiv(top, pivots[k])
    after, here = [], [y[ITERS - 1]]
    for k in range(ITERS - 2, -1, -1):
        out = [dneg(dmul(alphas[k], b)) for b in here] + [zero]
        out[0] = dadd(out[0], y[k])
        out[1] = dadd(out[1], here[0])
        for j in range(1, len(here)):
            half = dscale(here[j], 0.5)
            out[j + 1] = dadd(out[j + 1], half)
            out[j - 1] = dadd(out[j - 1], half)
        for j, b in enumerate(after):
            out[j] = dsub(out[j], dmul(betas[k + 1], b))
        after, here = here, out
    return [c[0] for c in here]


def shifted_rows(load, k, tiles, step):
    r = k * SUBS + step
    if r < 0 or r + SUBS > tiles * SUBS:
        return pltpu.roll(load(k * SUBS), (-step) % SUBS, 0)
    return load(r)


def shifted_lanes(centers, lane):
    count = len(centers)
    lower = [pltpu.roll(c, LANES - 1, 1) for c in centers]
    upper = [pltpu.roll(c, 1, 1) for c in centers]
    east = [jnp.where(lane == LANES - 1, lower[(t + 1) % count], lower[t]) for t in range(count)]
    west = [jnp.where(lane == 0, upper[t - 1], upper[t]) for t in range(count)]
    return east, west


def build_basis(
    raw, cells, pairs, got_a, got_b, got_c, got_d,
    basis, scaled, message, links, diag, inverse, leak, sums,
):
    row_even = lax.rem(lax.axis_index("rows"), 2) == 0
    col_even = lax.rem(lax.axis_index("cols"), 2) == 0
    planes, spans, high, _ = raw.shape
    fields = planes - 2
    demes = fields // 2
    tiles = high // SUBS
    rows, cols = high - 2 * SUBS, (spans - 1) * LANES
    lane = lane_iota()
    zero = jnp.zeros((SUBS, LANES), jnp.float32)

    def plane(f):
        if f < fields:
            return lambda t, r, v: basis.__setitem__((0, f, t, r, slice(None)), v)
        target = leak if f == fields else scaled
        return lambda t, r, v: target.__setitem__((t, r, slice(None)), v)

    for f in range(fields + 2):
        store = plane(f)
        size = ITERS + (f == fields + 1)
        for t in range(spans - 1):
            store(t, slice(SUBS, SUBS + rows), raw[f, t, SUBS : SUBS + rows, :])
            north, south = halo_rows(row_even, got_a, got_b, f * ITERS, size, t * LANES, (t + 1) * LANES)
            store(t, slice(0, SUBS), zero)
            store(t, slice(SUBS + rows, 2 * SUBS + rows), zero)
            store(t, slice(SUBS - size, SUBS), north)
            store(t, slice(SUBS + rows, SUBS + rows + size), south)
    for k in range(tiles):
        r = slice(k * SUBS, (k + 1) * SUBS)
        from_c, from_d = got_c[r, :], got_d[r, :]
        east = jnp.where(col_even, from_c, from_d)
        west = jnp.where(col_even, from_d, from_c)
        for f in range(fields + 2):
            size = ITERS + (f == fields + 1)
            first = pltpu.roll(east, (-f * ITERS) % LANES, 1) if f else east
            final = pltpu.roll(west, (LANES - size - f * ITERS) % LANES, 1)
            value = jnp.where(lane < size, first, jnp.where(lane >= LANES - size, final, 0.0))
            plane(f)(spans - 1, r, value)

    total_cols = cols * lax.axis_size("cols")
    for j in range(demes):
        cell = cells[j]
        row = lax.div(cell, total_cols) - lax.axis_index("rows") * rows
        col = lax.rem(cell, total_cols) - lax.axis_index("cols") * cols

        @pl.when((row >= -ITERS) & (row < rows + ITERS) & (col >= -ITERS) & (col < cols + ITERS))
        def _():
            spot = jnp.where(col < 0, col + spans * LANES, col)
            tile = lax.div(spot, LANES)
            at = spot - tile * LANES
            line = basis[0, demes + j, tile, pl.ds(row + SUBS, 1), :]
            here = lax.broadcasted_iota(jnp.int32, (1, LANES), 1) == at
            basis[0, demes + j, tile, pl.ds(row + SUBS, 1), :] = line + jnp.where(here, 4.0, 0.0)

    for k in range(tiles):
        r = slice(k * SUBS, (k + 1) * SUBS)
        centers = [scaled[t, r, :] for t in range(spans)]
        easts, wests = shifted_lanes(centers, lane)
        for t in range(spans):
            load = lambda at: scaled[t, at : at + SUBS, :]
            here = centers[t]
            others = [
                shifted_rows(load, k, tiles, 1), shifted_rows(load, k, tiles, -1), easts[t], wests[t],
            ]
            twice = [jnp.where(jnp.minimum(here, o) > 0.0, here + o, 0.0) for o in others]
            d = leak[t, r, :] + 0.5 * (twice[0] + twice[1] + twice[2] + twice[3])
            inv = jnp.where(d > 0.0, 1.0 / jnp.where(d > 0.0, d, 1.0), 0.0)
            for side in range(4):
                links[side, t, r, :] = twice[side] * inv
            diag[t, r, :] = d
            inverse[t, r, :] = jnp.where(here > 0.0, inv, 0.0)

    def finish(k, carry):
        r = pl.ds(pl.multiple_of(k * SUBS, SUBS), SUBS)
        for t in range(spans):
            inv = inverse[t, r, :]
            for f in range(demes):
                basis[0, f, t, r, :] = basis[0, f, t, r, :] * inv
            readout = [basis[0, demes + j, t, r, :] * inv for j in range(demes)]
            for f in range(demes):
                total = pairs[f, 0] * readout[0]
                for j in range(1, demes):
                    total = total + pairs[f, j] * readout[j]
                basis[0, demes + f, t, r, :] = total
        return carry

    lax.fori_loop(0, tiles, finish, 0)

    for step in range(ITERS):
        for k in range(tiles):
            own_rows = 0 < k < tiles - 1
            if step == ITERS - 1 and not own_rows:
                continue
            r = slice(k * SUBS, (k + 1) * SUBS)
            weights = [[links[side, t, r, :] for side in range(4)] for t in range(spans)]
            if step == 0:
                weights = [[0.5 * w for w in ws] for ws in weights]
            ds = [diag[t, r, :] for t in range(spans - 1)] if own_rows else None

            def field(f, carry, step=step, k=k, own_rows=own_rows, r=r, weights=weights, ds=ds):
                centers = [basis[step, f, t, r, :] for t in range(spans)]
                easts, wests = shifted_lanes(centers, lane)
                first = second = None
                for t in range(spans):
                    halo = t == spans - 1
                    if step == ITERS - 1 and halo:
                        continue
                    load = lambda at: basis[step, f, t, at : at + SUBS, :]
                    south = shifted_rows(load, k, tiles, 1)
                    north = shifted_rows(load, k, tiles, -1)
                    w = weights[t]
                    value = (w[0] * south + w[1] * north) + (w[2] * easts[t] + w[3] * wests[t])
                    if step:
                        value = value - basis[step - 1, f, t, r, :]
                    if step < ITERS - 1:
                        basis[step + 1, f, t, r, :] = value
                    if own_rows and not halo:
                        e = ds[t] * centers[t]
                        one, two = e * centers[t], e * value
                        first = one if first is None else first + one
                        second = two if second is None else second + two
                if own_rows:
                    if k == 1:
                        sums[2 * step, f] = first
                        sums[2 * step + 1, f] = second
                    else:
                        sums[2 * step, f] += first
                        sums[2 * step + 1, f] += second
                return carry

            lax.fori_loop(0, fields, field, 0, unroll=fields)

    packed = zero
    for m in range(2 * ITERS):
        for half in range(2):
            value = jnp.sum(sums[m, half * demes : (half + 1) * demes], axis=1)
            high, low = value, zero
            shift = LANES // 2
            while shift:
                high, low = dadd((high, low), (pltpu.roll(high, shift, 1), pltpu.roll(low, shift, 1)))
                shift //= 2
            at = half * (LANES // 2) + m
            packed = jnp.where(lane == at, high, jnp.where(lane == at + 16, low, packed))
    message[...] = jnp.broadcast_to(packed[None], message.shape)


def combine(everyone, basis, scaled, solution, grad, potential, values, sems):
    devices = everyone.shape[0]
    fields, rows, cols = solution.shape
    demes = fields // 2
    spans = cols // LANES + 1
    tiles = rows // SUBS + 2
    lane = lane_iota()
    zero = jnp.zeros((SUBS, LANES), jnp.float32)
    chains = [(everyone[i], zero) for i in range(4)]
    for i in range(4, devices):
        high, low = chains[i % 4]
        s, e = two_sum(high, everyone[i])
        chains[i % 4] = (s, low + e)
    total = dadd(dadd(*(quick(*c) for c in chains[:2])), dadd(*(quick(*c) for c in chains[2:])))
    total = dadd(total, tuple(pltpu.roll(part, LANES - 16, 1) for part in total))
    raw = [total] + [
        tuple(pltpu.roll(part, LANES - m, 1) for part in total) for m in range(1, 2 * ITERS)
    ]
    mu = raw[:2] + [dsub(dscale(raw[m], 2.0), raw[m % 2]) for m in range(2, 2 * ITERS)]
    coefficients = polynomial(mu)

    flows = []
    for f in range(fields):
        half, sub = divmod(f, demes)
        lo = half * (LANES // 2)
        c = [jnp.broadcast_to(v[sub : sub + 1, lo : lo + 1], (SUBS, LANES)) for v in coefficients]
        for k in range(tiles):
            r = slice(k * SUBS, (k + 1) * SUBS)
            own_rows = 0 < k < tiles - 1
            for t in range(spans if own_rows else spans - 1):
                value = c[0] * basis[0, f, t, r, :]
                for j in range(1, ITERS):
                    value = value + c[j] * basis[j, f, t, r, :]
                potential[f, t, r, :] = value
                if own_rows and t < spans - 1:
                    values[f, (k - 1) * SUBS : k * SUBS, t * LANES : (t + 1) * LANES] = value
        flows.append(pltpu.make_async_copy(values.at[f], solution.at[f], sems.at[f]))
        flows[-1].start()

    def gradient(k, carry):
        base = pl.multiple_of(k * SUBS, SUBS)
        r = pl.ds(base, SUBS)
        totals = [[zero] * 4 for _ in range(spans - 1)]
        for f in range(demes):
            differ = []
            for g in (f, demes + f):
                centers = [potential[g, t, r, :] for t in range(spans)]
                easts, wests = shifted_lanes(centers, lane)
                differ.append(
                    [
                        (
                            centers[t] - potential[g, t, pl.ds(base + 1, SUBS), :],
                            centers[t] - potential[g, t, pl.ds(base - 1, SUBS), :],
                            centers[t] - easts[t],
                            centers[t] - wests[t],
                        )
                        for t in range(spans - 1)
                    ]
                )
            for t in range(spans - 1):
                for side in range(4):
                    totals[t][side] = totals[t][side] + differ[0][t][side] * differ[1][t][side]
        centers = [scaled[t, r, :] for t in range(spans)]
        easts, wests = shifted_lanes(centers, lane)
        for t in range(spans - 1):
            others = [
                scaled[t, pl.ds(base + 1, SUBS), :], scaled[t, pl.ds(base - 1, SUBS), :], easts[t], wests[t],
            ]
            value = zero
            for side in range(4):
                linked = jnp.minimum(centers[t], others[side]) > 0.0
                value = value + jnp.where(linked, totals[t][side], 0.0)
            grad[pl.ds(base - SUBS, SUBS), t * LANES : (t + 1) * LANES] = -0.5 * value
        return carry

    lax.fori_loop(1, tiles - 1, gradient, 0)
    for flow in flows:
        flow.wait()


def on_device(sources, sample_maps, conductance, shunt, nodata_mask, deme_cells, pair_weights):
    demes, rows, cols = sources.shape
    fields = 2 * demes
    spans = cols // LANES + 1
    high = rows + 2 * SUBS
    slab = -(-((fields + 2) * ITERS + 1) // SUBS) * SUBS
    f32 = jnp.float32
    params = pltpu.CompilerParams(vmem_limit_bytes=LIMIT)
    block = [
        pltpu.with_memory_space_constraint(x, pltpu.HBM)
        for x in (sources, sample_maps, conductance, shunt, nodata_mask)
    ]
    count_r, count_c = lax.axis_size("rows"), lax.axis_size("cols")

    send_a, send_b, raw = pl.pallas_call(
        pack_rows,
        out_shape=[jax.ShapeDtypeStruct((slab, cols), f32)] * 2
        + [pltpu.VMEM((fields + 2, spans, high, LANES), f32)],
        in_specs=[pl.BlockSpec(memory_space=pltpu.HBM)] * 5,
        out_specs=[VMEM] * 3,
        scratch_shapes=[
            pltpu.VMEM((2, fields, SUBS, cols), f32),
            pltpu.VMEM((2, rows, cols), f32),
            pltpu.VMEM((rows, cols), jnp.int32),
            pltpu.SemaphoreType.DMA((7 + 2 * (spans - 1),)),
        ],
        compiler_params=params,
        name="pack_rows",
    )(*block)
    got_a = lax.ppermute(send_a, "rows", swaps(count_r, 0))
    got_b = lax.ppermute(send_b, "rows", swaps(count_r, 1))
    send_c, send_d = pl.pallas_call(
        pack_cols,
        out_shape=[jax.ShapeDtypeStruct((high, LANES), f32)] * 2,
        in_specs=[VMEM] * 3,
        out_specs=[VMEM] * 2,
        scratch_shapes=[pltpu.VMEM((2, fields + 2, 2 * SUBS, LANES), f32)],
        compiler_params=params,
        name="pack_cols",
    )(raw, got_a, got_b)
    got_c = lax.ppermute(send_c, "cols", swaps(count_c, 0))
    got_d = lax.ppermute(send_d, "cols", swaps(count_c, 1))

    everyone = count_r * count_c
    basis, scaled, message = pl.pallas_call(
        build_basis,
        out_shape=[
            pltpu.VMEM((ITERS, fields, spans, high, LANES), f32),
            pltpu.VMEM((spans, high, LANES), f32),
            jax.ShapeDtypeStruct((everyone, SUBS, LANES), f32),
        ],
        in_specs=[VMEM] + [SMEM] * 2 + [VMEM] * 4,
        out_specs=[VMEM] * 3,
        scratch_shapes=[
            pltpu.VMEM((4, spans, high, LANES), f32),
            pltpu.VMEM((spans, high, LANES), f32),
            pltpu.VMEM((spans, high, LANES), f32),
            pltpu.VMEM((spans, high, LANES), f32),
            pltpu.VMEM((2 * ITERS, fields, SUBS, LANES), f32),
        ],
        compiler_params=params,
        name="build_basis",
    )(raw, deme_cells, pair_weights, got_a, got_b, got_c, got_d)
    gathered = lax.all_to_all(message, ("rows", "cols"), 0, 0)
    return pl.pallas_call(
        combine,
        out_shape=[
            jax.ShapeDtypeStruct((fields, rows, cols), f32),
            jax.ShapeDtypeStruct((rows, cols), f32),
        ],
        in_specs=[VMEM] * 3,
        out_specs=[pl.BlockSpec(memory_space=pltpu.HBM), VMEM],
        scratch_shapes=[
            pltpu.VMEM((fields, spans, high, LANES), f32),
            pltpu.VMEM((fields, rows, cols), f32),
            pltpu.SemaphoreType.DMA((fields,)),
        ],
        compiler_params=params,
        name="combine",
    )(gathered, basis, scaled)


def solution(mesh):
    return jax.shard_map(
        on_device,
        mesh=mesh,
        in_specs=(
            P(None, "rows", "cols"),
            P(None, "rows", "cols"),
            P("rows", "cols"),
            P("rows", "cols"),
            P("rows", "cols"),
            P(),
            P(),
        ),
        out_specs=(P(None, "rows", "cols"), P("rows", "cols")),
        check_vma=False,
    )
```

```python
import functools

import jax
import jax.numpy as jnp
from jax import lax
from jax.experimental import pallas as pl
from jax.experimental.pallas import tpu as pltpu
from jax.sharding import PartitionSpec as P

ITERS = 5
LANES = 128
SUBS = 8
VMEM = pl.BlockSpec(memory_space=pltpu.VMEM)
SMEM = pl.BlockSpec(memory_space=pltpu.SMEM)
LIMIT = 40 * 1024 * 1024


def swaps(count, first):
    pairs = [(i, i + 1) for i in range(first, count - 1, 2)]
    return pairs + [(b, a) for a, b in pairs]


def lane_iota():
    return lax.broadcasted_iota(jnp.int32, (SUBS, LANES), 1)


def scaled_of(conductance, mask):
    return jnp.where(mask != 0, conductance, 0.0)


def first_and_cols(
    src, maps, cond, shunt, mask, cells_in, pairs_in, raw, c_out, d_out, pairs, cells, flats, masks, sems
):
    col_even = lax.rem(lax.axis_index("cols"), 2) == 0
    rows, cols = cond.shape
    demes = src.shape[0]
    fields = 2 * demes
    planes = fields + 2
    spans = cols // LANES
    flows = []

    def fetch(source, target):
        flow = pltpu.make_async_copy(source, target, sems.at[len(flows)])
        flow.start()
        flows.append(flow)

    fetch(cells_in, cells)
    fetch(cond, flats)
    fetch(mask, masks)
    fetch(pairs_in, pairs)
    order = [0, spans - 1] + list(range(1, spans - 1))
    for t in order:
        c = slice(t * LANES, (t + 1) * LANES)
        own = slice(SUBS, SUBS + rows)
        fetch(src.at[:, :, c], raw.at[0:demes, t, own, :])
        fetch(maps.at[:, :, c], raw.at[demes:fields, t, own, :])
        fetch(shunt.at[:, c], raw.at[fields, t, own, :])
    for flow in flows:
        flow.wait()
    for t in range(spans):
        c = slice(t * LANES, (t + 1) * LANES)
        raw[fields + 1, t, SUBS : SUBS + rows, :] = scaled_of(flats[:, c], masks[:, c])
    lane = lane_iota()
    total_cols = cols * lax.axis_size("cols")
    for j in range(demes):
        cell = cells[j]
        row = lax.div(cell, total_cols) - lax.axis_index("rows") * rows
        col = lax.rem(cell, total_cols) - lax.axis_index("cols") * cols

        @pl.when((row >= 0) & (row < rows) & (col >= 0) & (col < cols))
        def _():
            tile = lax.div(col, LANES)
            line = raw[demes + j, tile, pl.ds(row + SUBS, 1), :]
            here = lax.broadcasted_iota(jnp.int32, (1, LANES), 1) == col - tile * LANES
            raw[demes + j, tile, pl.ds(row + SUBS, 1), :] = line + jnp.where(here, 4.0, 0.0)

    for k in range(rows // SUBS):
        both = []
        for side, t in enumerate((0, spans - 1)):
            total = jnp.zeros((SUBS, LANES), jnp.float32)
            for f in range(planes):
                size = ITERS + (f == planes - 1)
                piece = raw[f, t, (k + 1) * SUBS : (k + 2) * SUBS, :]
                start = 0 if side == 0 else LANES - size
                shift = (f * ITERS - start) % LANES
                moved = pltpu.roll(piece, shift, 1) if shift else piece
                keep = (lane >= f * ITERS) & (lane < f * ITERS + size)
                total = jnp.where(keep, moved, total)
            both.append(total)
        west, east = both
        r = slice(k * SUBS, (k + 1) * SUBS)
        c_out[r, :] = jnp.where(col_even, east, west)
        d_out[r, :] = jnp.where(col_even, west, east)


def pack_rows(raw, got_c, got_d, a_out, b_out):
    even = lax.rem(lax.axis_index("rows"), 2) == 0
    planes, spans, high, _ = raw.shape
    end = high - SUBS
    for f in range(planes):
        size = ITERS + (f == planes - 1)
        at = f * ITERS
        for t in range(spans - 1):
            north, south = raw[f, t, SUBS : SUBS + size, :], raw[f, t, end - size : end, :]
            c = slice(t * LANES, (t + 1) * LANES)
            a_out[at : at + size, c] = jnp.where(even, south, north)
            b_out[at : at + size, c] = jnp.where(even, north, south)
    corner = a_out.shape[0] - SUBS
    rows = got_c.shape[0]
    for i, got in enumerate((got_c, got_d)):
        north, south = got[0:SUBS, :], got[rows - SUBS : rows, :]
        c = slice(i * LANES, (i + 1) * LANES)
        a_out[corner : corner + SUBS, c] = jnp.where(even, south, north)
        b_out[corner : corner + SUBS, c] = jnp.where(even, north, south)


def halo_rows(even, got_a, got_b, at, size, lo, hi):
    a = got_a[at : at + size, lo:hi]
    b = got_b[at : at + size, lo:hi]
    return jnp.where(even, b, a), jnp.where(even, a, b)


def two_sum(a, b):
    s = a + b
    t = s - a
    return s, (a - (s - t)) + (b - t)


def quick(a, b):
    s = a + b
    return s, b - (s - a)


def split(a):
    c = 4097.0 * a
    high = c - (c - a)
    return high, a - high


def two_prod(a, b):
    p = a * b
    ah, al = split(a)
    bh, bl = split(b)
    return p, ((ah * bh - p) + ah * bl + al * bh) + al * bl


def dadd(x, y):
    s, e = two_sum(x[0], y[0])
    return quick(s, e + (x[1] + y[1]))


def dneg(x):
    return -x[0], -x[1]


def dsub(x, y):
    return dadd(x, dneg(y))


def dmul(x, y):
    p, e = two_prod(x[0], y[0])
    return quick(p, e + (x[0] * y[1] + x[1] * y[0]))


def dscale(x, power_of_two):
    return x[0] * power_of_two, x[1] * power_of_two


def ddiv(x, y):
    q = x[0] / y[0]
    p, e = two_prod(q, y[0])
    rest = (x[0] - p) - e + x[1] - q * y[1]
    return quick(q, rest / y[0])


def dclamp(x, low, high):
    h = jnp.where(x[0] < low, low, jnp.where(x[0] > high, high, x[0]))
    return h, jnp.where(h == x[0], x[1], 0.0)


def polynomial(mu):
    zero = (jnp.zeros_like(mu[0][0]), jnp.zeros_like(mu[0][0]))
    one = (jnp.ones_like(mu[0][0]), zero[0])
    before, now = None, {l: mu[l] for l in range(2 * ITERS)}
    alphas, betas = [], [None]
    ratio_before, norm_before = None, None
    for k in range(ITERS):
        norm = (jnp.maximum(now[k][0], 1e-30), jnp.where(now[k][0] > 1e-30, now[k][1], 0.0))
        ratio = ddiv(now[k + 1], norm)
        if k:
            ratio = dscale(ratio, 0.5)
            beta = ddiv(norm, norm_before)
            if k > 1:
                beta = dscale(beta, 0.5)
            betas.append(dclamp(beta, 0.0, 1.0))
        alpha = ratio if k == 0 else dsub(ratio, ratio_before)
        alphas.append(dclamp(alpha, -1.0, 1.0))
        ratio_before, norm_before = ratio, norm
        if k == ITERS - 1:
            break
        following = {}
        for l in range(k + 1, 2 * ITERS - 1 - k):
            value = dadd(now[l + 1], now[l - 1]) if l - 1 >= k else now[l + 1]
            value = dsub(dscale(value, 0.5), dmul(alphas[k], now[l]))
            if k:
                value = dsub(value, dmul(betas[k], before[l]))
            following[l] = value
        before, now = now, following
    pivots, gains = [], []
    for k in range(ITERS):
        pivot = dsub(one, alphas[k])
        gain = one
        if k:
            pivot = dsub(pivot, ddiv(betas[k], pivots[-1]))
            gain = ddiv(gains[-1], pivots[-1])
        pivots.append(dclamp(pivot, 1e-6, 4.0))
        gains.append(gain)
    y = [None] * ITERS
    for k in range(ITERS - 1, -1, -1):
        top = gains[k] if k == ITERS - 1 else dadd(gains[k], dmul(betas[k + 1], y[k + 1]))
        y[k] = ddiv(top, pivots[k])
    after, here = [], [y[ITERS - 1]]
    for k in range(ITERS - 2, -1, -1):
        out = [dneg(dmul(alphas[k], b)) for b in here] + [zero]
        out[0] = dadd(out[0], y[k])
        out[1] = dadd(out[1], here[0])
        for j in range(1, len(here)):
            half = dscale(here[j], 0.5)
            out[j + 1] = dadd(out[j + 1], half)
            out[j - 1] = dadd(out[j - 1], half)
        for j, b in enumerate(after):
            out[j] = dsub(out[j], dmul(betas[k + 1], b))
        after, here = here, out
    return [c[0] for c in here]


def shifted_rows(load, k, tiles, step):
    r = k * SUBS + step
    if r < 0 or r + SUBS > tiles * SUBS:
        return pltpu.roll(load(k * SUBS), (-step) % SUBS, 0)
    return load(r)


def shifted_east(centers, lane):
    count = len(centers)
    lower = [pltpu.roll(c, LANES - 1, 1) for c in centers]
    return [jnp.where(lane == LANES - 1, lower[(t + 1) % count], lower[t]) for t in range(count)]


def shifted_lanes(centers, lane):
    count = len(centers)
    lower = [pltpu.roll(c, LANES - 1, 1) for c in centers]
    upper = [pltpu.roll(c, 1, 1) for c in centers]
    east = [jnp.where(lane == LANES - 1, lower[(t + 1) % count], lower[t]) for t in range(count)]
    west = [jnp.where(lane == 0, upper[t - 1], upper[t]) for t in range(count)]
    return east, west


class Block:
    def __init__(self, raw, pairs, got_c, got_d, basis, scaled, links, diag, inverse, leak, sums):
        self.raw, self.pairs, self.got_c, self.got_d = raw, pairs, got_c, got_d
        self.basis, self.scaled, self.links, self.diag = basis, scaled, links, diag
        self.inverse, self.leak, self.sums = inverse, leak, sums
        planes, self.spans, high, _ = raw.shape
        self.fields = planes - 2
        self.demes = self.fields // 2
        self.tiles = high // SUBS
        self.rows, self.cols = high - 2 * SUBS, (self.spans - 1) * LANES
        self.lane = lane_iota()

    def store(self, f, t, r, value):
        if f < self.fields:
            self.basis[0, f, t, r, :] = value
        elif f == self.fields:
            self.leak[t, r, :] = value
        else:
            self.scaled[t, r, :] = value

    def own(self, k):
        return 0 < k < self.tiles - 1

    def fill(self, ks, planes, got_a=None, got_b=None):
        col_even = lax.rem(lax.axis_index("cols"), 2) == 0
        row_even = lax.rem(lax.axis_index("rows"), 2) == 0
        for k in ks:
            r = slice(k * SUBS, (k + 1) * SUBS)
            if self.own(k):
                m = slice((k - 1) * SUBS, k * SUBS)
                from_c, from_d = self.got_c[m, :], self.got_d[m, :]
            else:
                corner = got_a.shape[0] - SUBS
                pieces = []
                for i in range(2):
                    both = halo_rows(row_even, got_a, got_b, corner, SUBS, i * LANES, (i + 1) * LANES)
                    pieces.append(both[0 if k == 0 else 1])
                from_c, from_d = pieces
            east = jnp.where(col_even, from_c, from_d)
            west = jnp.where(col_even, from_d, from_c)
            for f in planes:
                size = ITERS + (f == self.fields + 1)
                for t in range(self.spans - 1):
                    if self.own(k):
                        if f >= self.fields:
                            self.store(f, t, r, self.raw[f, t, r, :])
                        continue
                    self.store(f, t, r, jnp.zeros((SUBS, LANES), jnp.float32))
                    north, south = halo_rows(
                        row_even, got_a, got_b, f * ITERS, size, t * LANES, (t + 1) * LANES
                    )
                    if k == 0:
                        self.store(f, t, slice(SUBS - size, SUBS), north)
                    else:
                        self.store(f, t, slice(k * SUBS, k * SUBS + size), south)
                first = pltpu.roll(east, (-f * ITERS) % LANES, 1) if f else east
                final = pltpu.roll(west, (LANES - size - f * ITERS) % LANES, 1)
                value = jnp.where(self.lane < size, first, jnp.where(self.lane >= LANES - size, final, 0.0))
                self.store(f, self.spans - 1, r, value)

    def weights(self, ks):
        for k in ks:
            r = slice(k * SUBS, (k + 1) * SUBS)
            centers = [self.scaled[t, r, :] for t in range(self.spans)]
            easts, wests = shifted_lanes(centers, self.lane)
            for t in range(self.spans):
                load = lambda at: self.scaled[t, at : at + SUBS, :]
                here = centers[t]
                others = [
                    shifted_rows(load, k, self.tiles, 1), shifted_rows(load, k, self.tiles, -1),
                    easts[t], wests[t],
                ]
                twice = [jnp.where(jnp.minimum(here, o) > 0.0, here + o, 0.0) for o in others]
                d = self.leak[t, r, :] + 0.5 * (twice[0] + twice[1] + twice[2] + twice[3])
                inv = jnp.where(d > 0.0, 1.0 / jnp.where(d > 0.0, d, 1.0), 0.0)
                for side in range(4):
                    self.links[side, t, r, :] = twice[side] * inv
                self.diag[t, r, :] = d
                self.inverse[t, r, :] = jnp.where(here > 0.0, inv, 0.0)

    def finish(self, ks):
        for k in ks:
            r = slice(k * SUBS, (k + 1) * SUBS)
            for t in range(self.spans):
                inv = self.inverse[t, r, :]
                ready = self.raw if self.own(k) and t < self.spans - 1 else self.basis.at[0]
                for f in range(self.demes):
                    self.basis[0, f, t, r, :] = ready[f, t, r, :] * inv
                readout = [ready[self.demes + j, t, r, :] * inv for j in range(self.demes)]
                for f in range(self.demes):
                    total = self.pairs[f, 0] * readout[0]
                    for j in range(1, self.demes):
                        total = total + self.pairs[f, j] * readout[j]
                    self.basis[0, self.demes + f, t, r, :] = total

    def steps(self, ks, summed, skipped, fresh):
        basis, sums, spans = self.basis, self.sums, self.spans

        def add(at, f, value, k):
            if fresh and k == summed[0]:
                sums[at, f] = value
            else:
                sums[at, f] += value

        for step in range(ITERS):
            final = step == ITERS - 1
            for k in ks:
                adds = k in summed
                if (final and not adds) or (step == ITERS - 2 and k in skipped):
                    continue
                r = slice(k * SUBS, (k + 1) * SUBS)
                ds = [self.diag[t, r, :] for t in range(spans - 1)] if adds else None
                weights = [[self.links[side, t, r, :] for side in range(4)] for t in range(spans)]
                if step == 0:
                    weights = [[0.5 * w for w in ws] for ws in weights]
                for f in range(self.fields):
                    centers = [basis[step, f, t, r, :] for t in range(spans)]
                    first = second = None
                    if final:
                        easts = shifted_east(centers, self.lane)
                    else:
                        easts, wests = shifted_lanes(centers, self.lane)
                    for t in range(spans):
                        halo = t == spans - 1
                        if final and halo:
                            continue
                        load = lambda at: basis[step, f, t, at : at + SUBS, :]
                        south = shifted_rows(load, k, self.tiles, 1)
                        w = weights[t]
                        if final:
                            value = w[0] * south + w[2] * easts[t]
                        else:
                            north = shifted_rows(load, k, self.tiles, -1)
                            value = (w[0] * south + w[1] * north) + (w[2] * easts[t] + w[3] * wests[t])
                            if step:
                                value = value - basis[step - 1, f, t, r, :]
                            basis[step + 1, f, t, r, :] = value
                        if adds and not halo:
                            e = ds[t] * centers[t]
                            one, two = e * centers[t], e * value
                            first = one if first is None else first + one
                            second = two if second is None else second + two
                    if adds:
                        add(2 * step, f, first, k)
                        add(2 * step + 1, f, second, k)


def inner_rows(raw, pairs, got_c, got_d, basis, sums, scaled, links, diag, inverse, leak):
    block = Block(raw, pairs, got_c, got_d, basis, scaled, links, diag, inverse, leak, sums)
    ks = list(range(1, block.tiles - 1))
    block.fill(ks, range(block.fields + 2))
    block.weights(ks)
    block.finish(ks)
    block.steps(ks, ks[1:-1], ks[:1], True)


def outer_rows(
    raw, pairs, got_c, got_d, got_a, got_b, basis_in, sums_in,
    basis, scaled, message, sums, links, diag, inverse, leak,
):
    block = Block(raw, pairs, got_c, got_d, basis, scaled, links, diag, inverse, leak, sums)
    ks = [0, 1, block.tiles - 2, block.tiles - 1]
    sums[...] = sums_in[...]
    block.fill(range(block.tiles), [block.fields + 1], got_a, got_b)
    block.fill(ks, range(block.fields + 1), got_a, got_b)
    block.weights(ks)
    block.finish(ks)
    block.steps(ks, ks[1:-1], (), False)

    lane, demes = block.lane, block.demes
    packed = zero = jnp.zeros((SUBS, LANES), jnp.float32)
    for m in range(2 * ITERS):
        for half in range(2):
            value = jnp.sum(sums[m, half * demes : (half + 1) * demes], axis=1)
            high, low = value, zero
            shift = LANES // 2
            while shift:
                high, low = dadd((high, low), (pltpu.roll(high, shift, 1), pltpu.roll(low, shift, 1)))
                shift //= 2
            at = half * (LANES // 2) + m
            packed = jnp.where(lane == at, high, jnp.where(lane == at + 16, low, packed))
    half = SUBS // 2
    message[...] = jnp.broadcast_to(
        jnp.where(lane[:half] % 64 < 32, packed[:half], pltpu.roll(packed, 32, 1)[half:])[None], message.shape
    )


def combine(everyone, basis, scaled, solution, grad, potential, across, sems):
    devices = everyone.shape[0]
    fields, rows, cols = solution.shape
    demes = fields // 2
    spans = cols // LANES + 1
    tiles = rows // SUBS + 2
    lane = lane_iota()
    zero = jnp.zeros((SUBS, LANES), jnp.float32)
    chains = [(everyone[i], zero[: SUBS // 2]) for i in range(4)]
    for i in range(4, devices):
        high, low = chains[i % 4]
        s, e = two_sum(high, everyone[i])
        chains[i % 4] = (s, low + e)
    total = dadd(dadd(*(quick(*c) for c in chains[:2])), dadd(*(quick(*c) for c in chains[2:])))
    total = tuple(jnp.concatenate([part, part], axis=0) for part in total)
    sub = lax.broadcasted_iota(jnp.int32, (SUBS, LANES), 0)
    total = tuple(jnp.where(sub < SUBS // 2, part, pltpu.roll(part, LANES - 32, 1)) for part in total)
    total = dadd(total, tuple(pltpu.roll(part, LANES - 16, 1) for part in total))
    raw = [total] + [
        tuple(pltpu.roll(part, LANES - m, 1) for part in total) for m in range(1, 2 * ITERS)
    ]
    mu = raw[:2] + [dsub(dscale(raw[m], 2.0), raw[m % 2]) for m in range(2, 2 * ITERS - 1)]
    tail = dadd(mu[2 * ITERS - 3], dscale(mu[1], 2.0))
    mu.append(dsub(dscale(raw[2 * ITERS - 1], 4.0), tail))
    coefficients = polynomial(mu)

    flows = []
    group = 4
    for f in range(fields):
        half, sub = divmod(f, demes)
        lo = half * (LANES // 2)
        c = [jnp.broadcast_to(v[sub : sub + 1, lo : lo + 1], (SUBS, LANES)) for v in coefficients]
        for k in range(tiles):
            r = slice(k * SUBS, (k + 1) * SUBS)
            own_rows = 0 < k < tiles - 1
            for t in range(spans if own_rows else spans - 1):
                value = c[0] * basis[0, f, t, r, :]
                for j in range(1, ITERS):
                    value = value + c[j] * basis[j, f, t, r, :]
                potential[f, t, r, :] = value
        if f % group == group - 1:
            g = slice(f + 1 - group, f + 1)
            for t in range(spans - 1):
                flow = pltpu.make_async_copy(
                    potential.at[g, t, SUBS : SUBS + rows, :],
                    solution.at[g, :, t * LANES : (t + 1) * LANES],
                    sems.at[len(flows)],
                )
                flow.start()
                flows.append(flow)

    for k in range(tiles - 1):
        r = slice(k * SUBS, (k + 1) * SUBS)
        below = slice(k * SUBS + 1, (k + 1) * SUBS + 1)
        down = [None] * (spans - 1)
        right = [None] * spans
        for f in range(demes):
            differ = []
            for g in (f, demes + f):
                centers = [potential[g, t, r, :] for t in range(spans)]
                steps = [centers[t] - potential[g, t, below, :] for t in range(spans - 1)]
                if k:
                    easts = shifted_east(centers, lane)
                    steps += [centers[t] - easts[t] for t in range(spans)]
                differ.append(steps)
            products = [a * b for a, b in zip(*differ)]
            for t in range(spans - 1):
                down[t] = products[t] if f == 0 else down[t] + products[t]
            for t in range(spans if k else 0):
                value = products[spans - 1 + t]
                right[t] = value if f == 0 else right[t] + value
        centers = [scaled[t, r, :] for t in range(spans)]
        for t in range(spans - 1):
            linked = jnp.minimum(centers[t], scaled[t, below, :]) > 0.0
            across[t, r, :] = jnp.where(linked, down[t], 0.0)
        if k:
            easts = shifted_east(centers, lane)
            right = [
                jnp.where(jnp.minimum(centers[t], easts[t]) > 0.0, right[t], 0.0) for t in range(spans)
            ]
            turned = [pltpu.roll(v, 1, 1) for v in right]
            above = slice(k * SUBS - 1, (k + 1) * SUBS - 1)
            for t in range(spans - 1):
                left = jnp.where(lane == 0, turned[t - 1], turned[t])
                value = (across[t, r, :] + across[t, above, :]) + (right[t] + left)
                grad[(k - 1) * SUBS : k * SUBS, t * LANES : (t + 1) * LANES] = -0.5 * value
    for flow in flows:
        flow.wait()


def on_device(sources, sample_maps, conductance, shunt, nodata_mask, deme_cells, pair_weights):
    demes, rows, cols = sources.shape
    fields = 2 * demes
    spans = cols // LANES + 1
    high = rows + 2 * SUBS
    slab = -(-((fields + 2) * ITERS + 1) // SUBS) * SUBS
    f32 = jnp.float32
    params = pltpu.CompilerParams(vmem_limit_bytes=LIMIT)
    block = [
        pltpu.with_memory_space_constraint(x, pltpu.HBM)
        for x in (sources, sample_maps, conductance, shunt, nodata_mask, deme_cells, pair_weights)
    ]
    count_r, count_c = lax.axis_size("rows"), lax.axis_size("cols")

    raw, send_c, send_d, pairs = pl.pallas_call(
        first_and_cols,
        out_shape=[pltpu.VMEM((fields + 2, spans, high, LANES), f32)]
        + [jax.ShapeDtypeStruct((rows, LANES), f32)] * 2
        + [pltpu.SMEM(pair_weights.shape, f32)],
        in_specs=[pl.BlockSpec(memory_space=pltpu.HBM)] * 7,
        out_specs=[VMEM] * 3 + [SMEM],
        scratch_shapes=[
            pltpu.SMEM(deme_cells.shape, jnp.int32),
            pltpu.VMEM((rows, cols), f32),
            pltpu.VMEM((rows, cols), jnp.int32),
            pltpu.SemaphoreType.DMA((4 + 3 * (spans - 1),)),
        ],
        compiler_params=params,
        name="first_and_cols",
    )(*block)
    got_c = lax.ppermute(send_c, "cols", swaps(count_c, 0))
    got_d = lax.ppermute(send_d, "cols", swaps(count_c, 1))
    send_a, send_b = pl.pallas_call(
        pack_rows,
        out_shape=[jax.ShapeDtypeStruct((slab + SUBS, cols), f32)] * 2,
        in_specs=[VMEM] * 3,
        out_specs=[VMEM] * 2,
        compiler_params=params,
        name="pack_rows",
    )(raw, got_c, got_d)
    got_a = lax.ppermute(send_a, "rows", swaps(count_r, 0))
    got_b = lax.ppermute(send_b, "rows", swaps(count_r, 1))

    everyone = count_r * count_c
    basis_shape = pltpu.VMEM((ITERS, fields, spans, high, LANES), f32)
    sums_shape = pltpu.VMEM((2 * ITERS, fields, SUBS, LANES), f32)
    plane = pltpu.VMEM((spans, high, LANES), f32)
    flat = [pltpu.VMEM((4, spans, high, LANES), f32)] + [plane] * 3
    basis, sums = pl.pallas_call(
        inner_rows,
        out_shape=[basis_shape, sums_shape],
        in_specs=[VMEM, SMEM] + [VMEM] * 2,
        out_specs=[VMEM] * 2,
        scratch_shapes=[plane] + flat,
        compiler_params=params,
        cost_estimate=pl.CostEstimate(flops=40_000_000, bytes_accessed=20_000_000, transcendentals=0),
        name="inner_rows",
    )(raw, pairs, got_c, got_d)
    basis, scaled, message = pl.pallas_call(
        outer_rows,
        out_shape=[basis_shape, plane, jax.ShapeDtypeStruct((everyone, SUBS // 2, LANES), f32)],
        in_specs=[VMEM, SMEM] + [VMEM] * 6,
        out_specs=[VMEM] * 3,
        scratch_shapes=[sums_shape] + flat,
        input_output_aliases={6: 0},
        compiler_params=params,
        name="outer_rows",
    )(raw, pairs, got_c, got_d, got_a, got_b, basis, sums)
    gathered = lax.all_to_all(message, ("rows", "cols"), 0, 0)
    return pl.pallas_call(
        combine,
        out_shape=[
            jax.ShapeDtypeStruct((fields, rows, cols), f32),
            jax.ShapeDtypeStruct((rows, cols), f32),
        ],
        in_specs=[VMEM] * 3,
        out_specs=[pl.BlockSpec(memory_space=pltpu.HBM), VMEM],
        scratch_shapes=[
            pltpu.VMEM((fields, spans, high, LANES), f32),
            plane,
            pltpu.SemaphoreType.DMA((fields // 4 * (spans - 1),)),
        ],
        compiler_params=params,
        name="combine",
    )(gathered, basis, scaled)


def solution(mesh):
    return jax.shard_map(
        on_device,
        mesh=mesh,
        in_specs=(
            P(None, "rows", "cols"),
            P(None, "rows", "cols"),
            P("rows", "cols"),
            P("rows", "cols"),
            P("rows", "cols"),
            P(),
            P(),
        ),
        out_specs=(P(None, "rows", "cols"), P("rows", "cols")),
        check_vma=False,
    )
```

```python
import functools

import jax
import jax.numpy as jnp
from jax import lax
from jax.experimental import pallas as pl
from jax.experimental.pallas import tpu as pltpu
from jax.sharding import PartitionSpec as P

ITERS = 5
LANES = 128
SUBS = 8
VMEM = pl.BlockSpec(memory_space=pltpu.VMEM)
LIMIT = 40 * 1024 * 1024


def swaps(count, first):
    pairs = [(i, i + 1) for i in range(first, count - 1, 2)]
    return pairs + [(b, a) for a, b in pairs]


def lane_iota():
    return lax.broadcasted_iota(jnp.int32, (SUBS, LANES), 1)


def scaled_of(conductance, mask):
    return jnp.where(mask != 0, conductance, 0.0)


def first_and_cols(
    src, maps, cond, shunt, mask, cells_in, pairs_in, raw, c_out, d_out, cells, pairs, flats, masks, sems
):
    col_even = lax.rem(lax.axis_index("cols"), 2) == 0
    rows, cols = cond.shape
    demes = src.shape[0]
    fields = 2 * demes
    planes = fields + 2
    spans = cols // LANES
    flows = []

    def fetch(source, target):
        flow = pltpu.make_async_copy(source, target, sems.at[len(flows)])
        flow.start()
        flows.append(flow)

    fetch(cells_in, cells)
    fetch(cond, flats)
    fetch(mask, masks)
    fetch(pairs_in, pairs)
    heads = len(flows)
    order = [0, spans - 1] + list(range(1, spans - 1))
    for t in order:
        c = slice(t * LANES, (t + 1) * LANES)
        own = slice(SUBS, SUBS + rows)
        fetch(src.at[:, :, c], raw.at[0:demes, t, own, :])
        fetch(maps.at[:, :, c], raw.at[demes:fields, t, own, :])
        fetch(shunt.at[:, c], raw.at[fields, t, own, :])
    for flow in flows[:heads]:
        flow.wait()
    lane = lane_iota()
    total_cols = cols * lax.axis_size("cols")
    for i, t in enumerate(order):
        for flow in flows[heads + 3 * i : heads + 3 * (i + 1)]:
            flow.wait()
        c = slice(t * LANES, (t + 1) * LANES)
        raw[fields + 1, t, SUBS : SUBS + rows, :] = scaled_of(flats[:, c], masks[:, c])
        for j in range(demes):
            cell = cells[j]
            row = lax.div(cell, total_cols) - lax.axis_index("rows") * rows
            col = lax.rem(cell, total_cols) - lax.axis_index("cols") * cols - t * LANES

            @pl.when((row >= 0) & (row < rows) & (col >= 0) & (col < LANES))
            def _():
                line = raw[demes + j, t, pl.ds(row + SUBS, 1), :]
                here = lax.broadcasted_iota(jnp.int32, (1, LANES), 1) == col
                raw[demes + j, t, pl.ds(row + SUBS, 1), :] = line + jnp.where(here, 4.0, 0.0)

        for k in range(1, rows // SUBS + 1):
            r = slice(k * SUBS, (k + 1) * SUBS)
            readout = [raw[demes + j, t, r, :] for j in range(demes)]
            for f in range(demes):
                total = pairs[f, 0] * readout[0]
                for j in range(1, demes):
                    total = total + pairs[f, j] * readout[j]
                raw[demes + f, t, r, :] = total
    for k in range(rows // SUBS):
        both = []
        for side, t in enumerate((0, spans - 1)):
            total = jnp.zeros((SUBS, LANES), jnp.float32)
            for f in range(planes):
                size = ITERS + (f == planes - 1)
                piece = raw[f, t, (k + 1) * SUBS : (k + 2) * SUBS, :]
                start = 0 if side == 0 else LANES - size
                shift = (f * ITERS - start) % LANES
                moved = pltpu.roll(piece, shift, 1) if shift else piece
                keep = (lane >= f * ITERS) & (lane < f * ITERS + size)
                total = jnp.where(keep, moved, total)
            both.append(total)
        west, east = both
        r = slice(k * SUBS, (k + 1) * SUBS)
        c_out[r, :] = jnp.where(col_even, east, west)
        d_out[r, :] = jnp.where(col_even, west, east)


def pack_rows(raw, got_c, got_d, a_out, b_out):
    even = lax.rem(lax.axis_index("rows"), 2) == 0
    planes, spans, high, _ = raw.shape
    end = high - SUBS
    for f in range(planes):
        size = ITERS + (f == planes - 1)
        at = SUBS + f * ITERS
        for t in range(spans - 1):
            north, south = raw[f, t, SUBS : SUBS + size, :], raw[f, t, end - size : end, :]
            c = slice(t * LANES, (t + 1) * LANES)
            a_out[at : at + size, c] = jnp.where(even, south, north)
            b_out[at : at + size, c] = jnp.where(even, north, south)
    rows = got_c.shape[0]
    for i, got in enumerate((got_c, got_d)):
        north, south = got[0:SUBS, :], got[rows - SUBS : rows, :]
        c = slice(i * LANES, (i + 1) * LANES)
        a_out[0:SUBS, c] = jnp.where(even, south, north)
        b_out[0:SUBS, c] = jnp.where(even, north, south)


def two_sum(a, b):
    s = a + b
    t = s - a
    return s, (a - (s - t)) + (b - t)


def quick(a, b):
    s = a + b
    return s, b - (s - a)


def split(a):
    c = 4097.0 * a
    high = c - (c - a)
    return high, a - high


def two_prod(a, b):
    p = a * b
    ah, al = split(a)
    bh, bl = split(b)
    return p, ((ah * bh - p) + ah * bl + al * bh) + al * bl


def dadd(x, y):
    s, e = two_sum(x[0], y[0])
    return quick(s, e + (x[1] + y[1]))


def dneg(x):
    return -x[0], -x[1]


def dsub(x, y):
    return dadd(x, dneg(y))


def dmul(x, y):
    p, e = two_prod(x[0], y[0])
    return quick(p, e + (x[0] * y[1] + x[1] * y[0]))


def dscale(x, power_of_two):
    return x[0] * power_of_two, x[1] * power_of_two


def ddiv(x, y):
    q = x[0] / y[0]
    p, e = two_prod(q, y[0])
    rest = (x[0] - p) - e + x[1] - q * y[1]
    return quick(q, rest / y[0])


def dclamp(x, low, high):
    h = jnp.where(x[0] < low, low, jnp.where(x[0] > high, high, x[0]))
    return h, jnp.where(h == x[0], x[1], 0.0)


def polynomial(mu):
    zero = (jnp.zeros_like(mu[0][0]), jnp.zeros_like(mu[0][0]))
    one = (jnp.ones_like(mu[0][0]), zero[0])
    before, now = None, {l: mu[l] for l in range(2 * ITERS)}
    alphas, betas = [], [None]
    ratio_before, norm_before = None, None
    for k in range(ITERS):
        norm = (jnp.maximum(now[k][0], 1e-30), jnp.where(now[k][0] > 1e-30, now[k][1], 0.0))
        ratio = ddiv(now[k + 1], norm)
        if k:
            ratio = dscale(ratio, 0.5)
            beta = ddiv(norm, norm_before)
            if k > 1:
                beta = dscale(beta, 0.5)
            betas.append(dclamp(beta, 0.0, 1.0))
        alpha = ratio if k == 0 else dsub(ratio, ratio_before)
        alphas.append(dclamp(alpha, -1.0, 1.0))
        ratio_before, norm_before = ratio, norm
        if k == ITERS - 1:
            break
        following = {}
        for l in range(k + 1, 2 * ITERS - 1 - k):
            value = dadd(now[l + 1], now[l - 1]) if l - 1 >= k else now[l + 1]
            value = dsub(dscale(value, 0.5), dmul(alphas[k], now[l]))
            if k:
                value = dsub(value, dmul(betas[k], before[l]))
            following[l] = value
        before, now = now, following
    pivots, gains = [], []
    for k in range(ITERS):
        pivot = dsub(one, alphas[k])
        gain = one
        if k:
            pivot = dsub(pivot, ddiv(betas[k], pivots[-1]))
            gain = ddiv(gains[-1], pivots[-1])
        pivots.append(dclamp(pivot, 1e-6, 4.0))
        gains.append(gain)
    y = [None] * ITERS
    for k in range(ITERS - 1, -1, -1):
        top = gains[k] if k == ITERS - 1 else dadd(gains[k], dmul(betas[k + 1], y[k + 1]))
        y[k] = ddiv(top, pivots[k])
    after, here = [], [y[ITERS - 1]]
    for k in range(ITERS - 2, -1, -1):
        out = [dneg(dmul(alphas[k], b)) for b in here] + [zero]
        out[0] = dadd(out[0], y[k])
        out[1] = dadd(out[1], here[0])
        for j in range(1, len(here)):
            half = dscale(here[j], 0.5)
            out[j + 1] = dadd(out[j + 1], half)
            out[j - 1] = dadd(out[j - 1], half)
        for j, b in enumerate(after):
            out[j] = dsub(out[j], dmul(betas[k + 1], b))
        after, here = here, out
    return [c[0] for c in here]


def shifted_rows(load, k, tiles, step):
    r = k * SUBS + step
    if r < 0 or r + SUBS > tiles * SUBS:
        return pltpu.roll(load(k * SUBS), (-step) % SUBS, 0)
    return load(r)


def shifted_east(centers, lane):
    count = len(centers)
    lower = [pltpu.roll(c, LANES - 1, 1) for c in centers]
    return [jnp.where(lane == LANES - 1, lower[(t + 1) % count], lower[t]) for t in range(count)]


def shifted_lanes(centers, lane):
    count = len(centers)
    lower = [pltpu.roll(c, LANES - 1, 1) for c in centers]
    upper = [pltpu.roll(c, 1, 1) for c in centers]
    east = [jnp.where(lane == LANES - 1, lower[(t + 1) % count], lower[t]) for t in range(count)]
    west = [jnp.where(lane == 0, upper[t - 1], upper[t]) for t in range(count)]
    return east, west


class Block:
    def __init__(self, raw, got_c, got_d, basis, scaled, links, diag, inverse, leak, sums):
        self.raw, self.got_c, self.got_d = raw, got_c, got_d
        self.basis, self.scaled, self.links, self.diag = basis, scaled, links, diag
        self.inverse, self.leak, self.sums = inverse, leak, sums
        planes, self.spans, high, _ = raw.shape
        self.fields = planes - 2
        self.tiles = high // SUBS
        self.lane = lane_iota()
        self.sub = lax.broadcasted_iota(jnp.int32, (SUBS, LANES), 0)
        self.col_even = lax.rem(lax.axis_index("cols"), 2) == 0

    def own(self, k):
        return 0 < k < self.tiles - 1

    def columns(self, from_c, from_d, f):
        east = jnp.where(self.col_even, from_c, from_d)
        west = jnp.where(self.col_even, from_d, from_c)
        size = ITERS + (f == self.fields + 1)
        first = pltpu.roll(east, (-f * ITERS) % LANES, 1) if f else east
        final = pltpu.roll(west, (LANES - size - f * ITERS) % LANES, 1)
        return jnp.where(self.lane < size, first, jnp.where(self.lane >= LANES - size, final, 0.0))

    def fill(self, ks):
        for k in ks:
            r = slice(k * SUBS, (k + 1) * SUBS)
            m = slice((k - 1) * SUBS, k * SUBS)
            for f, target in ((self.fields, self.leak), (self.fields + 1, self.scaled)):
                for t in range(self.spans - 1):
                    target[t, r, :] = self.raw[f, t, r, :]
                target[self.spans - 1, r, :] = self.columns(self.got_c[m, :], self.got_d[m, :], f)

    def fill_halo(self, north, south):
        for f, target in ((self.fields, self.leak), (self.fields + 1, self.scaled)):
            size = ITERS + (f == self.fields + 1)
            at = SUBS + f * ITERS
            for k, slab, lo in ((0, north, at + size - SUBS), (self.tiles - 1, south, at)):
                r = slice(k * SUBS, (k + 1) * SUBS)
                for t in range(self.spans - 1):
                    target[t, r, :] = slab[lo : lo + SUBS, t * LANES : (t + 1) * LANES]
                pieces = [slab[0:SUBS, i * LANES : (i + 1) * LANES] for i in range(2)]
                target[self.spans - 1, r, :] = self.columns(*pieces, f)

    def merge(self, north, south):
        return jnp.where(self.sub < SUBS // 2, south, north)

    def beyond(self, north, south):
        return jnp.where(self.sub < SUBS // 2, south, north)

    def weights_halo(self):
        low, high = slice(0, SUBS), slice((self.tiles - 1) * SUBS, self.tiles * SUBS)
        invs = []
        for t in range(self.spans):
            for side in range(4):
                self.links[side, t, low, :] = self.merge(self.links[side, t, low, :], self.links[side, t, high, :])
            north, south = self.inverse[t, low, :], self.inverse[t, high, :]
            invs.append(
                (self.merge(north, south), self.beyond(pltpu.roll(north, 1, 0), pltpu.roll(south, SUBS - 1, 0)))
            )
        return invs

    def start_halo(self, north, south, extra):
        low, high = slice(0, SUBS), slice((self.tiles - 1) * SUBS, self.tiles * SUBS)
        invs = self.weights_halo()
        corners = [[slab[0:SUBS, i * LANES : (i + 1) * LANES] for i in range(2)] for slab in (north, south)]
        near = [self.merge(n, s) for n, s in zip(*corners)]
        far = [self.beyond(pltpu.roll(n, 1, 0), pltpu.roll(s, SUBS - 1, 0)) for n, s in zip(*corners)]
        for f in range(self.fields):
            at = SUBS + f * ITERS
            up = at + ITERS - SUBS
            for t in range(self.spans):
                c = slice(t * LANES, (t + 1) * LANES)
                if t < self.spans - 1:
                    one = self.merge(north[up : up + SUBS, c], south[at : at + SUBS, c])
                    two = self.beyond(north[up - 1 : up - 1 + SUBS, c], south[at + 1 : at + 1 + SUBS, c])
                else:
                    one, two = self.columns(*near, f), self.columns(*far, f)
                value = one * invs[t][0]
                self.basis[0, f, t, low, :] = value
                self.basis[0, f, t, high, :] = value
                extra[f, t] = two * invs[t][1]

    def weights(self, ks):
        for k in ks:
            r = slice(k * SUBS, (k + 1) * SUBS)
            centers = [self.scaled[t, r, :] for t in range(self.spans)]
            easts, wests = shifted_lanes(centers, self.lane)
            for t in range(self.spans):
                load = lambda at: self.scaled[t, at : at + SUBS, :]
                here = centers[t]
                others = [
                    shifted_rows(load, k, self.tiles, 1), shifted_rows(load, k, self.tiles, -1),
                    easts[t], wests[t],
                ]
                twice = [jnp.where(jnp.minimum(here, o) > 0.0, here + o, 0.0) for o in others]
                d = self.leak[t, r, :] + 0.5 * (twice[0] + twice[1] + twice[2] + twice[3])
                inv = jnp.where(d > 0.0, 1.0 / jnp.where(d > 0.0, d, 1.0), 0.0)
                for side in range(4):
                    self.links[side, t, r, :] = twice[side] * inv
                self.diag[t, r, :] = d
                self.inverse[t, r, :] = jnp.where(here > 0.0, inv, 0.0)

    def start(self, ks):
        for k in ks:
            r = slice(k * SUBS, (k + 1) * SUBS)
            m = slice((k - 1) * SUBS, k * SUBS)
            from_c, from_d = self.got_c[m, :], self.got_d[m, :]
            for t in range(self.spans):
                inv = self.inverse[t, r, :]
                for f in range(self.fields):
                    here = self.raw[f, t, r, :] if t < self.spans - 1 else self.columns(from_c, from_d, f)
                    self.basis[0, f, t, r, :] = here * inv

    def steps(self, ks, summed, skipped, fresh, extra=None):
        basis, sums, spans = self.basis, self.sums, self.spans

        def add(at, f, value, k):
            if fresh and k == summed[0]:
                sums[at, f] = value
            else:
                sums[at, f] += value

        for step in range(ITERS):
            final = step == ITERS - 1
            for k in ks:
                adds = k in summed
                if (final and not adds) or (step == ITERS - 2 and k in skipped):
                    continue
                r = slice(k * SUBS, (k + 1) * SUBS)
                ds = [self.diag[t, r, :] for t in range(spans - 1)] if adds else None
                weights = [[self.links[side, t, r, :] for side in range(4)] for t in range(spans)]
                if step == 0:
                    weights = [[0.5 * w for w in ws] for ws in weights]
                for f in range(self.fields):
                    centers = [basis[step, f, t, r, :] for t in range(spans)]
                    first = second = None
                    if final:
                        easts = shifted_east(centers, self.lane)
                    else:
                        easts, wests = shifted_lanes(centers, self.lane)
                    for t in range(spans):
                        halo = t == spans - 1
                        if final and halo:
                            continue
                        south = basis[step, f, t, k * SUBS + 1 : (k + 1) * SUBS + 1, :]
                        if k == 0 and step == 0:
                            south = jnp.where(self.sub == SUBS // 2 - 1, extra[f, t], south)
                        w = weights[t]
                        if final:
                            value = w[0] * south + w[2] * easts[t]
                        else:
                            at = k * SUBS if k else (self.tiles - 1) * SUBS
                            north = basis[step, f, t, at - 1 : at - 1 + SUBS, :]
                            if k == 0 and step == 0:
                                north = jnp.where(self.sub == SUBS // 2, extra[f, t], north)
                            value = (w[0] * south + w[1] * north) + (w[2] * easts[t] + w[3] * wests[t])
                            if step:
                                value = value - basis[step - 1, f, t, r, :]
                            basis[step + 1, f, t, r, :] = value
                            if k == 0:
                                basis[step + 1, f, t, (self.tiles - 1) * SUBS : self.tiles * SUBS, :] = value
                        if adds and not halo:
                            e = ds[t] * centers[t]
                            one, two = e * centers[t], e * value
                            first = one if first is None else first + one
                            second = two if second is None else second + two
                    if adds:
                        add(2 * step, f, first, k)
                        add(2 * step + 1, f, second, k)


def inner_rows(raw, got_c, got_d, basis, sums, scaled, links, diag, inverse, leak):
    block = Block(raw, got_c, got_d, basis, scaled, links, diag, inverse, leak, sums)
    ks = list(range(1, block.tiles - 1))
    block.fill(ks)
    block.weights(ks)
    block.start(ks)
    block.steps(ks, ks[1:-1], ks[:1], True)


def outer_rows(
    raw, got_c, got_d, got_a, got_b, basis_in, sums_in,
    basis, sums, scaled, message, links, diag, inverse, leak, extra,
):
    block = Block(raw, got_c, got_d, basis, scaled, links, diag, inverse, leak, sums)
    even = lax.rem(lax.axis_index("rows"), 2) == 0
    last = block.tiles - 1
    block.fill(range(1, last))

    def halo(north, south):
        block.fill_halo(north, south)
        block.weights([0, 1, last - 1, last])
        block.start_halo(north, south, extra)

    @pl.when(even)
    def _():
        halo(got_b, got_a)

    @pl.when(jnp.logical_not(even))
    def _():
        halo(got_a, got_b)

    block.start([1, last - 1])
    block.steps([0, 1, last - 1], [1, last - 1], (), False, extra)
    message[...] = jnp.broadcast_to(packed_sums(sums)[None], message.shape)


def folded(values, width, axis, unit):
    size = SUBS if axis == 0 else LANES
    at = lax.broadcasted_iota(jnp.int32, (SUBS, LANES), axis)
    first = lax.rem(at, 2 * width) < width
    out = []
    for i in range(0, len(values), 2):
        a = values[i]
        b = values[i + 1] if i + 1 < len(values) else a
        here = tuple(jnp.where(first, x, y) for x, y in zip(a, b))
        there = tuple(
            jnp.where(first, pltpu.roll(x, size - width, axis), pltpu.roll(y, width, axis)) for x, y in zip(a, b)
        )
        out.append(unit(here, there))
    return out


def packed_sums(sums):
    count, fields = sums.shape[:2]
    demes = fields // 2
    order = [int(format(s, "03b")[::-1], 2) for s in range(SUBS)]
    columns = []
    for m in range(count):
        for half in range(2):
            parts = [(sums[m, half * demes + s],) for s in order]
            for width in (4, 2, 1):
                parts = folded(parts, width, 0, lambda x, y: (x[0] + y[0],))
            columns.append(parts[0])
    parts = folded(columns, 64, 1, lambda x, y: two_sum(x[0], y[0]))
    for width in (32, 16, 8, 4, 2, 1):
        parts = folded(parts, width, 1, dadd)
    parts = parts[0]
    lane = lax.broadcasted_iota(jnp.int32, (SUBS, LANES), 1)
    both = jnp.where(lax.rem(lane, 2) == 0, parts[0], parts[1])
    half = SUBS // 2
    return jnp.where(lax.rem(lane[:half], 4) < 2, both[:half], pltpu.roll(both, 2, 1)[half:])


def spot(m):
    return 32 * (m & 1) + 16 * (m >> 1 & 1) + 8 * (m >> 2 & 1) + 4 * (m >> 3 & 1)


def combine(everyone, basis, scaled, solution, grad, potential, across, sems):
    devices = everyone.shape[0]
    fields, rows, cols = solution.shape
    demes = fields // 2
    spans = cols // LANES + 1
    tiles = rows // SUBS + 2
    lane = lane_iota()
    zero = jnp.zeros((SUBS, LANES), jnp.float32)
    chains = [(everyone[i], zero[: SUBS // 2]) for i in range(4)]
    for i in range(4, devices):
        high, low = chains[i % 4]
        s, e = two_sum(high, everyone[i])
        chains[i % 4] = (s, low + e)
    total = dadd(dadd(*(quick(*c) for c in chains[:2])), dadd(*(quick(*c) for c in chains[2:])))
    total = tuple(jnp.concatenate([part, part], axis=0) for part in total)
    sub = lax.broadcasted_iota(jnp.int32, (SUBS, LANES), 0)
    total = tuple(jnp.where(sub < SUBS // 2, part, pltpu.roll(part, LANES - 2, 1)) for part in total)
    total = dadd(total, tuple(pltpu.roll(part, LANES - 1, 1) for part in total))
    raw = [total] + [
        tuple(pltpu.roll(part, LANES - spot(m), 1) for part in total) for m in range(1, 2 * ITERS)
    ]
    mu = raw[:2] + [dsub(dscale(raw[m], 2.0), raw[m % 2]) for m in range(2, 2 * ITERS - 1)]
    tail = dadd(mu[2 * ITERS - 3], dscale(mu[1], 2.0))
    mu.append(dsub(dscale(raw[2 * ITERS - 1], 4.0), tail))
    coefficients = polynomial(mu)

    flows = []
    group = 4
    for f in range(fields):
        half, sub = divmod(f, demes)
        lo = half * (LANES // 2)
        c = [jnp.broadcast_to(v[sub : sub + 1, lo : lo + 1], (SUBS, LANES)) for v in coefficients]
        for k in range(tiles):
            r = slice(k * SUBS, (k + 1) * SUBS)
            own_rows = 0 < k < tiles - 1
            for t in range(spans if own_rows else spans - 1):
                value = c[0] * basis[0, f, t, r, :]
                for j in range(1, ITERS):
                    value = value + c[j] * basis[j, f, t, r, :]
                potential[f, t, r, :] = value
        if f % group == group - 1:
            g = slice(f + 1 - group, f + 1)
            for t in range(spans - 1):
                flow = pltpu.make_async_copy(
                    potential.at[g, t, SUBS : SUBS + rows, :],
                    solution.at[g, :, t * LANES : (t + 1) * LANES],
                    sems.at[len(flows)],
                )
                flow.start()
                flows.append(flow)

    for k in range(tiles - 1):
        r = slice(k * SUBS, (k + 1) * SUBS)
        below = slice(k * SUBS + 1, (k + 1) * SUBS + 1)
        down = [None] * (spans - 1)
        right = [None] * spans
        for f in range(demes):
            differ = []
            for g in (f, demes + f):
                centers = [potential[g, t, r, :] for t in range(spans)]
                steps = [centers[t] - potential[g, t, below, :] for t in range(spans - 1)]
                if k:
                    easts = shifted_east(centers, lane)
                    steps += [centers[t] - easts[t] for t in range(spans)]
                differ.append(steps)
            products = [a * b for a, b in zip(*differ)]
            for t in range(spans - 1):
                down[t] = products[t] if f == 0 else down[t] + products[t]
            for t in range(spans if k else 0):
                value = products[spans - 1 + t]
                right[t] = value if f == 0 else right[t] + value
        centers = [scaled[t, r, :] for t in range(spans)]
        for t in range(spans - 1):
            linked = jnp.minimum(centers[t], scaled[t, below, :]) > 0.0
            across[t, r, :] = jnp.where(linked, down[t], 0.0)
        if k:
            easts = shifted_east(centers, lane)
            right = [
                jnp.where(jnp.minimum(centers[t], easts[t]) > 0.0, right[t], 0.0) for t in range(spans)
            ]
            turned = [pltpu.roll(v, 1, 1) for v in right]
            above = slice(k * SUBS - 1, (k + 1) * SUBS - 1)
            for t in range(spans - 1):
                left = jnp.where(lane == 0, turned[t - 1], turned[t])
                value = (across[t, r, :] + across[t, above, :]) + (right[t] + left)
                grad[(k - 1) * SUBS : k * SUBS, t * LANES : (t + 1) * LANES] = -0.5 * value
    for flow in flows:
        flow.wait()


def on_device(sources, sample_maps, conductance, shunt, nodata_mask, deme_cells, pair_weights):
    demes, rows, cols = sources.shape
    fields = 2 * demes
    spans = cols // LANES + 1
    high = rows + 2 * SUBS
    slab = -(-((fields + 2) * ITERS + 1) // SUBS) * SUBS
    f32 = jnp.float32
    params = pltpu.CompilerParams(vmem_limit_bytes=LIMIT)
    block = [
        pltpu.with_memory_space_constraint(x, pltpu.HBM)
        for x in (sources, sample_maps, conductance, shunt, nodata_mask, deme_cells, pair_weights)
    ]
    count_r, count_c = lax.axis_size("rows"), lax.axis_size("cols")

    raw, send_c, send_d = pl.pallas_call(
        first_and_cols,
        out_shape=[pltpu.VMEM((fields + 2, spans, high, LANES), f32)]
        + [jax.ShapeDtypeStruct((rows, LANES), f32)] * 2,
        in_specs=[pl.BlockSpec(memory_space=pltpu.HBM)] * 7,
        out_specs=[VMEM] * 3,
        scratch_shapes=[
            pltpu.SMEM(deme_cells.shape, jnp.int32),
            pltpu.SMEM(pair_weights.shape, f32),
            pltpu.VMEM((rows, cols), f32),
            pltpu.VMEM((rows, cols), jnp.int32),
            pltpu.SemaphoreType.DMA((4 + 3 * (spans - 1),)),
        ],
        compiler_params=params,
        name="first_and_cols",
    )(*block)
    got_c = lax.ppermute(send_c, "cols", swaps(count_c, 0))
    got_d = lax.ppermute(send_d, "cols", swaps(count_c, 1))
    send_a, send_b = pl.pallas_call(
        pack_rows,
        out_shape=[jax.ShapeDtypeStruct((slab + SUBS, cols), f32)] * 2,
        in_specs=[VMEM] * 3,
        out_specs=[VMEM] * 2,
        compiler_params=params,
        name="pack_rows",
    )(raw, got_c, got_d)
    got_a = lax.ppermute(send_a, "rows", swaps(count_r, 0))
    got_b = lax.ppermute(send_b, "rows", swaps(count_r, 1))

    everyone = count_r * count_c
    basis_shape = pltpu.VMEM((ITERS, fields, spans, high, LANES), f32)
    sums_shape = pltpu.VMEM((2 * ITERS, fields, SUBS, LANES), f32)
    plane = pltpu.VMEM((spans, high, LANES), f32)
    flat = [pltpu.VMEM((4, spans, high, LANES), f32)] + [plane] * 3
    basis, sums = pl.pallas_call(
        inner_rows,
        out_shape=[basis_shape, sums_shape],
        in_specs=[VMEM] * 3,
        out_specs=[VMEM] * 2,
        scratch_shapes=[plane] + flat,
        compiler_params=params,
        cost_estimate=pl.CostEstimate(flops=40_000_000, bytes_accessed=20_000_000, transcendentals=0),
        name="inner_rows",
    )(raw, got_c, got_d)
    basis, _, scaled, message = pl.pallas_call(
        outer_rows,
        out_shape=[basis_shape, sums_shape, plane, jax.ShapeDtypeStruct((everyone, SUBS // 2, LANES), f32)],
        in_specs=[VMEM] * 7,
        out_specs=[VMEM] * 4,
        scratch_shapes=flat + [pltpu.VMEM((fields, spans, SUBS, LANES), f32)],
        input_output_aliases={5: 0, 6: 1},
        compiler_params=params,
        name="outer_rows",
    )(raw, got_c, got_d, got_a, got_b, basis, sums)
    gathered = lax.all_to_all(message, ("rows", "cols"), 0, 0)
    return pl.pallas_call(
        combine,
        out_shape=[
            jax.ShapeDtypeStruct((fields, rows, cols), f32),
            jax.ShapeDtypeStruct((rows, cols), f32),
        ],
        in_specs=[VMEM] * 3,
        out_specs=[pl.BlockSpec(memory_space=pltpu.HBM), VMEM],
        scratch_shapes=[
            pltpu.VMEM((fields, spans, high, LANES), f32),
            plane,
            pltpu.SemaphoreType.DMA((fields // 4 * (spans - 1),)),
        ],
        compiler_params=params,
        name="combine",
    )(gathered, basis, scaled)


def solution(mesh):
    return jax.shard_map(
        on_device,
        mesh=mesh,
        in_specs=(
            P(None, "rows", "cols"),
            P(None, "rows", "cols"),
            P("rows", "cols"),
            P("rows", "cols"),
            P("rows", "cols"),
            P(),
            P(),
        ),
        out_specs=(P(None, "rows", "cols"), P("rows", "cols")),
        check_vma=False,
    )
```

```python
import functools

import jax
import jax.numpy as jnp
from jax import lax
from jax.experimental import pallas as pl
from jax.experimental.pallas import tpu as pltpu
from jax.sharding import PartitionSpec as P

ITERS = 5
LANES = 128
SUBS = 8
VMEM = pl.BlockSpec(memory_space=pltpu.VMEM)
LIMIT = 40 * 1024 * 1024


def swaps(count, first):
    pairs = [(i, i + 1) for i in range(first, count - 1, 2)]
    return pairs + [(b, a) for a, b in pairs]


def lane_iota():
    return lax.broadcasted_iota(jnp.int32, (SUBS, LANES), 1)


def scaled_of(conductance, mask):
    return jnp.where(mask != 0, conductance, 0.0)


def first_and_cols(
    src, maps, cond, shunt, mask, cells_in, pairs_in, raw, c_out, d_out, cells, pairs, flats, masks, sems
):
    col_even = lax.rem(lax.axis_index("cols"), 2) == 0
    rows, cols = cond.shape
    demes = src.shape[0]
    fields = 2 * demes
    planes = fields + 2
    spans = cols // LANES
    flows = []

    def fetch(source, target):
        flow = pltpu.make_async_copy(source, target, sems.at[len(flows)])
        flow.start()
        flows.append(flow)

    fetch(cells_in, cells)
    fetch(cond, flats)
    fetch(mask, masks)
    fetch(pairs_in, pairs)
    heads = len(flows)
    order = [0, spans - 1] + list(range(1, spans - 1))
    for t in order:
        c = slice(t * LANES, (t + 1) * LANES)
        own = slice(SUBS, SUBS + rows)
        fetch(src.at[:, :, c], raw.at[0:demes, t, own, :])
        fetch(maps.at[:, :, c], raw.at[demes:fields, t, own, :])
        fetch(shunt.at[:, c], raw.at[fields, t, own, :])
    for flow in flows[:heads]:
        flow.wait()
    lane = lane_iota()
    total_cols = cols * lax.axis_size("cols")
    for i, t in enumerate(order):
        for flow in flows[heads + 3 * i : heads + 3 * (i + 1)]:
            flow.wait()
        c = slice(t * LANES, (t + 1) * LANES)
        raw[fields + 1, t, SUBS : SUBS + rows, :] = scaled_of(flats[:, c], masks[:, c])
        for j in range(demes):
            cell = cells[j]
            row = lax.div(cell, total_cols) - lax.axis_index("rows") * rows
            col = lax.rem(cell, total_cols) - lax.axis_index("cols") * cols - t * LANES

            @pl.when((row >= 0) & (row < rows) & (col >= 0) & (col < LANES))
            def _():
                line = raw[demes + j, t, pl.ds(row + SUBS, 1), :]
                here = lax.broadcasted_iota(jnp.int32, (1, LANES), 1) == col
                raw[demes + j, t, pl.ds(row + SUBS, 1), :] = line + jnp.where(here, 4.0, 0.0)

        for k in range(1, rows // SUBS + 1):
            r = slice(k * SUBS, (k + 1) * SUBS)
            readout = [raw[demes + j, t, r, :] for j in range(demes)]
            for f in range(demes):
                total = pairs[f, 0] * readout[0]
                for j in range(1, demes):
                    total = total + pairs[f, j] * readout[j]
                raw[demes + f, t, r, :] = total
    for k in range(rows // SUBS):
        both = []
        for side, t in enumerate((0, spans - 1)):
            total = jnp.zeros((SUBS, LANES), jnp.float32)
            for f in range(planes):
                size = ITERS + (f == planes - 1)
                piece = raw[f, t, (k + 1) * SUBS : (k + 2) * SUBS, :]
                start = 0 if side == 0 else LANES - size
                shift = (f * ITERS - start) % LANES
                moved = pltpu.roll(piece, shift, 1) if shift else piece
                keep = (lane >= f * ITERS) & (lane < f * ITERS + size)
                total = jnp.where(keep, moved, total)
            both.append(total)
        west, east = both
        r = slice(k * SUBS, (k + 1) * SUBS)
        c_out[r, :] = jnp.where(col_even, east, west)
        d_out[r, :] = jnp.where(col_even, west, east)


def pack_rows(raw, got_d, got_c, a_out, b_out):
    even = lax.rem(lax.axis_index("rows"), 2) == 0
    planes, spans, high, _ = raw.shape
    end = high - SUBS
    for f in range(planes):
        size = ITERS + (f == planes - 1)
        at = SUBS + f * ITERS
        for t in range(spans - 1):
            north, south = raw[f, t, SUBS : SUBS + size, :], raw[f, t, end - size : end, :]
            c = slice(t * LANES, (t + 1) * LANES)
            a_out[at : at + size, c] = jnp.where(even, south, north)
            b_out[at : at + size, c] = jnp.where(even, north, south)
    rows = got_c.shape[0]
    for i, got in enumerate((got_c, got_d)):
        north, south = got[0:SUBS, :], got[rows - SUBS : rows, :]
        c = slice(i * LANES, (i + 1) * LANES)
        a_out[0:SUBS, c] = jnp.where(even, south, north)
        b_out[0:SUBS, c] = jnp.where(even, north, south)


def two_sum(a, b):
    s = a + b
    t = s - a
    return s, (a - (s - t)) + (b - t)


def quick(a, b):
    s = a + b
    return s, b - (s - a)


def split(a):
    c = 4097.0 * a
    high = c - (c - a)
    return high, a - high


def two_prod(a, b):
    p = a * b
    ah, al = split(a)
    bh, bl = split(b)
    return p, ((ah * bh - p) + ah * bl + al * bh) + al * bl


def dadd(x, y):
    s, e = two_sum(x[0], y[0])
    return quick(s, e + (x[1] + y[1]))


def dneg(x):
    return -x[0], -x[1]


def dsub(x, y):
    return dadd(x, dneg(y))


def dmul(x, y):
    p, e = two_prod(x[0], y[0])
    return quick(p, e + (x[0] * y[1] + x[1] * y[0]))


def dscale(x, power_of_two):
    return x[0] * power_of_two, x[1] * power_of_two


def ddiv(x, y):
    q = x[0] / y[0]
    p, e = two_prod(q, y[0])
    rest = (x[0] - p) - e + x[1] - q * y[1]
    return quick(q, rest / y[0])


def dclamp(x, low, high):
    h = jnp.where(x[0] < low, low, jnp.where(x[0] > high, high, x[0]))
    return h, jnp.where(h == x[0], x[1], 0.0)


def polynomial(mu):
    zero = (jnp.zeros_like(mu[0][0]), jnp.zeros_like(mu[0][0]))
    one = (jnp.ones_like(mu[0][0]), zero[0])
    before, now = None, {l: mu[l] for l in range(2 * ITERS)}
    alphas, betas = [], [None]
    ratio_before, norm_before = None, None
    for k in range(ITERS):
        norm = (jnp.maximum(now[k][0], 1e-30), jnp.where(now[k][0] > 1e-30, now[k][1], 0.0))
        ratio = ddiv(now[k + 1], norm)
        if k:
            ratio = dscale(ratio, 0.5)
            beta = ddiv(norm, norm_before)
            if k > 1:
                beta = dscale(beta, 0.5)
            betas.append(dclamp(beta, 0.0, 1.0))
        alpha = ratio if k == 0 else dsub(ratio, ratio_before)
        alphas.append(dclamp(alpha, -1.0, 1.0))
        ratio_before, norm_before = ratio, norm
        if k == ITERS - 1:
            break
        following = {}
        for l in range(k + 1, 2 * ITERS - 1 - k):
            value = dadd(now[l + 1], now[l - 1]) if l - 1 >= k else now[l + 1]
            value = dsub(dscale(value, 0.5), dmul(alphas[k], now[l]))
            if k:
                value = dsub(value, dmul(betas[k], before[l]))
            following[l] = value
        before, now = now, following
    pivots, gains = [], []
    for k in range(ITERS):
        pivot = dsub(one, alphas[k])
        gain = one
        if k:
            pivot = dsub(pivot, ddiv(betas[k], pivots[-1]))
            gain = ddiv(gains[-1], pivots[-1])
        pivots.append(dclamp(pivot, 1e-6, 4.0))
        gains.append(gain)
    y = [None] * ITERS
    for k in range(ITERS - 1, -1, -1):
        top = gains[k] if k == ITERS - 1 else dadd(gains[k], dmul(betas[k + 1], y[k + 1]))
        y[k] = ddiv(top, pivots[k])
    after, here = [], [y[ITERS - 1]]
    for k in range(ITERS - 2, -1, -1):
        out = [dneg(dmul(alphas[k], b)) for b in here] + [zero]
        out[0] = dadd(out[0], y[k])
        out[1] = dadd(out[1], here[0])
        for j in range(1, len(here)):
            half = dscale(here[j], 0.5)
            out[j + 1] = dadd(out[j + 1], half)
            out[j - 1] = dadd(out[j - 1], half)
        for j, b in enumerate(after):
            out[j] = dsub(out[j], dmul(betas[k + 1], b))
        after, here = here, out
    return [c[0] for c in here]


def shifted_rows(load, k, tiles, step):
    r = k * SUBS + step
    if r < 0 or r + SUBS > tiles * SUBS:
        return pltpu.roll(load(k * SUBS), (-step) % SUBS, 0)
    return load(r)


def shifted_east(centers, lane):
    count = len(centers)
    lower = [pltpu.roll(c, LANES - 1, 1) for c in centers]
    return [jnp.where(lane == LANES - 1, lower[(t + 1) % count], lower[t]) for t in range(count)]


def shifted_lanes(centers, lane):
    count = len(centers)
    lower = [pltpu.roll(c, LANES - 1, 1) for c in centers]
    upper = [pltpu.roll(c, 1, 1) for c in centers]
    east = [jnp.where(lane == LANES - 1, lower[(t + 1) % count], lower[t]) for t in range(count)]
    west = [jnp.where(lane == 0, upper[t - 1], upper[t]) for t in range(count)]
    return east, west


class Block:
    def __init__(self, raw, got_c, got_d, basis, scaled, links, diag, inverse, leak, sums):
        self.raw, self.got_c, self.got_d = raw, got_c, got_d
        self.basis, self.scaled, self.links, self.diag = basis, scaled, links, diag
        self.inverse, self.leak, self.sums = inverse, leak, sums
        planes, self.spans, high, _ = raw.shape
        self.fields = planes - 2
        self.tiles = high // SUBS
        self.lane = lane_iota()
        self.sub = lax.broadcasted_iota(jnp.int32, (SUBS, LANES), 0)
        self.col_even = lax.rem(lax.axis_index("cols"), 2) == 0

    def own(self, k):
        return 0 < k < self.tiles - 1

    def columns(self, from_c, from_d, f):
        east = jnp.where(self.col_even, from_c, from_d)
        west = jnp.where(self.col_even, from_d, from_c)
        size = ITERS + (f == self.fields + 1)
        first = pltpu.roll(east, (-f * ITERS) % LANES, 1) if f else east
        final = pltpu.roll(west, (LANES - size - f * ITERS) % LANES, 1)
        return jnp.where(self.lane < size, first, jnp.where(self.lane >= LANES - size, final, 0.0))

    def fill(self, ks):
        for k in ks:
            r = slice(k * SUBS, (k + 1) * SUBS)
            m = slice((k - 1) * SUBS, k * SUBS)
            for f, target in ((self.fields, self.leak), (self.fields + 1, self.scaled)):
                for t in range(self.spans - 1):
                    target[t, r, :] = self.raw[f, t, r, :]
                target[self.spans - 1, r, :] = self.columns(self.got_c[m, :], self.got_d[m, :], f)

    def fill_halo(self, north, south):
        for f, target in ((self.fields, self.leak), (self.fields + 1, self.scaled)):
            size = ITERS + (f == self.fields + 1)
            at = SUBS + f * ITERS
            for k, slab, lo in ((0, north, at + size - SUBS), (self.tiles - 1, south, at)):
                r = slice(k * SUBS, (k + 1) * SUBS)
                for t in range(self.spans - 1):
                    target[t, r, :] = slab[lo : lo + SUBS, t * LANES : (t + 1) * LANES]
                pieces = [slab[0:SUBS, i * LANES : (i + 1) * LANES] for i in range(2)]
                target[self.spans - 1, r, :] = self.columns(*pieces, f)

    def merge(self, north, south):
        return jnp.where(self.sub < SUBS // 2, south, north)

    def beyond(self, north, south):
        return jnp.where(self.sub < SUBS // 2, south, north)

    def weights_halo(self):
        low, high = slice(0, SUBS), slice((self.tiles - 1) * SUBS, self.tiles * SUBS)
        invs = []
        for t in range(self.spans):
            for side in range(4):
                self.links[side, t, low, :] = self.merge(self.links[side, t, low, :], self.links[side, t, high, :])
            north, south = self.inverse[t, low, :], self.inverse[t, high, :]
            invs.append(
                (self.merge(north, south), self.beyond(pltpu.roll(north, 1, 0), pltpu.roll(south, SUBS - 1, 0)))
            )
        return invs

    def start_halo(self, north, south, extra):
        low, high = slice(0, SUBS), slice((self.tiles - 1) * SUBS, self.tiles * SUBS)
        invs = self.weights_halo()
        corners = [[slab[0:SUBS, i * LANES : (i + 1) * LANES] for i in range(2)] for slab in (north, south)]
        near = [self.merge(n, s) for n, s in zip(*corners)]
        far = [self.beyond(pltpu.roll(n, 1, 0), pltpu.roll(s, SUBS - 1, 0)) for n, s in zip(*corners)]
        for f in range(self.fields):
            at = SUBS + f * ITERS
            up = at + ITERS - SUBS
            for t in range(self.spans):
                c = slice(t * LANES, (t + 1) * LANES)
                if t < self.spans - 1:
                    one = self.merge(north[up : up + SUBS, c], south[at : at + SUBS, c])
                    two = self.beyond(north[up - 1 : up - 1 + SUBS, c], south[at + 1 : at + 1 + SUBS, c])
                else:
                    one, two = self.columns(*near, f), self.columns(*far, f)
                value = one * invs[t][0]
                self.basis[0, f, t, low, :] = value
                self.basis[0, f, t, high, :] = value
                extra[f, t] = two * invs[t][1]

    def weights(self, ks):
        for k in ks:
            r = slice(k * SUBS, (k + 1) * SUBS)
            centers = [self.scaled[t, r, :] for t in range(self.spans)]
            easts, wests = shifted_lanes(centers, self.lane)
            for t in range(self.spans):
                load = lambda at: self.scaled[t, at : at + SUBS, :]
                here = centers[t]
                others = [
                    shifted_rows(load, k, self.tiles, 1), shifted_rows(load, k, self.tiles, -1),
                    easts[t], wests[t],
                ]
                twice = [jnp.where(jnp.minimum(here, o) > 0.0, here + o, 0.0) for o in others]
                d = self.leak[t, r, :] + 0.5 * (twice[0] + twice[1] + twice[2] + twice[3])
                inv = jnp.where(d > 0.0, 1.0 / jnp.where(d > 0.0, d, 1.0), 0.0)
                for side in range(4):
                    self.links[side, t, r, :] = twice[side] * inv
                self.diag[t, r, :] = d
                self.inverse[t, r, :] = jnp.where(here > 0.0, inv, 0.0)

    def start(self, ks):
        for k in ks:
            r = slice(k * SUBS, (k + 1) * SUBS)
            m = slice((k - 1) * SUBS, k * SUBS)
            from_c, from_d = self.got_c[m, :], self.got_d[m, :]
            for t in range(self.spans):
                inv = self.inverse[t, r, :]
                for f in range(self.fields):
                    here = self.raw[f, t, r, :] if t < self.spans - 1 else self.columns(from_c, from_d, f)
                    self.basis[0, f, t, r, :] = here * inv

    def steps(self, ks, summed, skipped, fresh, extra=None):
        basis, sums, spans = self.basis, self.sums, self.spans

        def add(at, f, value, k):
            if fresh and k == summed[0]:
                sums[at, f] = value
            else:
                sums[at, f] += value

        for step in range(ITERS):
            final = step == ITERS - 1
            for k in ks:
                adds = k in summed
                if (final and not adds) or (step == ITERS - 2 and k in skipped):
                    continue
                r = slice(k * SUBS, (k + 1) * SUBS)
                ds = [self.diag[t, r, :] for t in range(spans - 1)] if adds else None
                weights = [[self.links[side, t, r, :] for side in range(4)] for t in range(spans)]
                if step == 0:
                    weights = [[0.5 * w for w in ws] for ws in weights]
                for f in range(self.fields):
                    centers = [basis[step, f, t, r, :] for t in range(spans)]
                    first = second = None
                    if final:
                        easts = shifted_east(centers, self.lane)
                    else:
                        easts, wests = shifted_lanes(centers, self.lane)
                    for t in range(spans):
                        halo = t == spans - 1
                        if final and halo:
                            continue
                        south = basis[step, f, t, k * SUBS + 1 : (k + 1) * SUBS + 1, :]
                        if k == 0 and step == 0:
                            south = jnp.where(self.sub == SUBS // 2 - 1, extra[f, t], south)
                        w = weights[t]
                        if final:
                            value = w[0] * south + w[2] * easts[t]
                        else:
                            at = k * SUBS if k else (self.tiles - 1) * SUBS
                            north = basis[step, f, t, at - 1 : at - 1 + SUBS, :]
                            if k == 0 and step == 0:
                                north = jnp.where(self.sub == SUBS // 2, extra[f, t], north)
                            value = (w[0] * south + w[1] * north) + (w[2] * easts[t] + w[3] * wests[t])
                            if step:
                                value = value - basis[step - 1, f, t, r, :]
                            basis[step + 1, f, t, r, :] = value
                            if k == 0:
                                basis[step + 1, f, t, (self.tiles - 1) * SUBS : self.tiles * SUBS, :] = value
                        if adds and not halo:
                            e = ds[t] * centers[t]
                            one, two = e * centers[t], e * value
                            first = one if first is None else first + one
                            second = two if second is None else second + two
                    if adds:
                        add(2 * step, f, first, k)
                        add(2 * step + 1, f, second, k)


def inner_rows(raw, got_d, got_c, basis, sums, scaled, links, diag, inverse, leak):
    block = Block(raw, got_c, got_d, basis, scaled, links, diag, inverse, leak, sums)
    ks = list(range(1, block.tiles - 1))
    block.fill(ks)
    block.weights(ks)
    block.start(ks)
    block.steps(ks, ks[1:-1], ks[:1], True)


def outer_rows(
    raw, got_d, got_c, got_b, got_a, basis_in, sums_in,
    basis, sums, scaled, message, links, diag, inverse, leak, extra,
):
    block = Block(raw, got_c, got_d, basis, scaled, links, diag, inverse, leak, sums)
    even = lax.rem(lax.axis_index("rows"), 2) == 0
    last = block.tiles - 1
    block.fill(range(1, last))

    def halo(north, south):
        block.fill_halo(north, south)
        block.weights([0, 1, last - 1, last])
        block.start_halo(north, south, extra)

    @pl.when(even)
    def _():
        halo(got_b, got_a)

    @pl.when(jnp.logical_not(even))
    def _():
        halo(got_a, got_b)

    block.start([1, last - 1])
    block.steps([0, 1, last - 1], [1, last - 1], (), False, extra)
    message[...] = jnp.broadcast_to(packed_sums(sums)[None], message.shape)


def folded(values, width, axis, unit):
    size = SUBS if axis == 0 else LANES
    at = lax.broadcasted_iota(jnp.int32, (SUBS, LANES), axis)
    first = lax.rem(at, 2 * width) < width
    out = []
    for i in range(0, len(values), 2):
        a = values[i]
        b = values[i + 1] if i + 1 < len(values) else a
        here = tuple(jnp.where(first, x, y) for x, y in zip(a, b))
        there = tuple(
            jnp.where(first, pltpu.roll(x, size - width, axis), pltpu.roll(y, width, axis)) for x, y in zip(a, b)
        )
        out.append(unit(here, there))
    return out


def packed_sums(sums):
    count, fields = sums.shape[:2]
    demes = fields // 2
    order = [int(format(s, "03b")[::-1], 2) for s in range(SUBS)]
    columns = []
    for m in range(count):
        for half in range(2):
            parts = [(sums[m, half * demes + s],) for s in order]
            for width in (4, 2, 1):
                parts = folded(parts, width, 0, lambda x, y: (x[0] + y[0],))
            columns.append(parts[0])
    parts = folded(columns, 64, 1, lambda x, y: two_sum(x[0], y[0]))
    for width in (32, 16, 8, 4, 2, 1):
        parts = folded(parts, width, 1, dadd)
    parts = parts[0]
    lane = lax.broadcasted_iota(jnp.int32, (SUBS, LANES), 1)
    both = jnp.where(lax.rem(lane, 2) == 0, parts[0], parts[1])
    half = SUBS // 2
    return jnp.where(lax.rem(lane[:half], 4) < 2, both[:half], pltpu.roll(both, 2, 1)[half:])


def spot(m):
    return 32 * (m & 1) + 16 * (m >> 1 & 1) + 8 * (m >> 2 & 1) + 4 * (m >> 3 & 1)


def combine(everyone, basis, scaled, solution, grad, potential, across, sems):
    devices = everyone.shape[0]
    fields, rows, cols = solution.shape
    demes = fields // 2
    spans = cols // LANES + 1
    tiles = rows // SUBS + 2
    lane = lane_iota()
    zero = jnp.zeros((SUBS, LANES), jnp.float32)
    chains = [(everyone[i], zero[: SUBS // 2]) for i in range(4)]
    for i in range(4, devices):
        high, low = chains[i % 4]
        s, e = two_sum(high, everyone[i])
        chains[i % 4] = (s, low + e)
    total = dadd(dadd(*(quick(*c) for c in chains[:2])), dadd(*(quick(*c) for c in chains[2:])))
    total = tuple(jnp.concatenate([part, part], axis=0) for part in total)
    sub = lax.broadcasted_iota(jnp.int32, (SUBS, LANES), 0)
    total = tuple(jnp.where(sub < SUBS // 2, part, pltpu.roll(part, LANES - 2, 1)) for part in total)
    total = dadd(total, tuple(pltpu.roll(part, LANES - 1, 1) for part in total))
    raw = [total] + [
        tuple(pltpu.roll(part, LANES - spot(m), 1) for part in total) for m in range(1, 2 * ITERS)
    ]
    mu = raw[:2] + [dsub(dscale(raw[m], 2.0), raw[m % 2]) for m in range(2, 2 * ITERS - 1)]
    tail = dadd(mu[2 * ITERS - 3], dscale(mu[1], 2.0))
    mu.append(dsub(dscale(raw[2 * ITERS - 1], 4.0), tail))
    coefficients = polynomial(mu)

    flows = []
    group = 4
    for f in range(fields):
        half, sub = divmod(f, demes)
        lo = half * (LANES // 2)
        c = [jnp.broadcast_to(v[sub : sub + 1, lo : lo + 1], (SUBS, LANES)) for v in coefficients]
        for k in range(tiles):
            r = slice(k * SUBS, (k + 1) * SUBS)
            own_rows = 0 < k < tiles - 1
            for t in range(spans if own_rows else spans - 1):
                value = c[0] * basis[0, f, t, r, :]
                for j in range(1, ITERS):
                    value = value + c[j] * basis[j, f, t, r, :]
                potential[f, t, r, :] = value
        if f % group == group - 1:
            g = slice(f + 1 - group, f + 1)
            for t in range(spans - 1):
                flow = pltpu.make_async_copy(
                    potential.at[g, t, SUBS : SUBS + rows, :],
                    solution.at[g, :, t * LANES : (t + 1) * LANES],
                    sems.at[len(flows)],
                )
                flow.start()
                flows.append(flow)

    for k in range(tiles - 1):
        r = slice(k * SUBS, (k + 1) * SUBS)
        below = slice(k * SUBS + 1, (k + 1) * SUBS + 1)
        down = [None] * (spans - 1)
        right = [None] * spans
        for f in range(demes):
            differ = []
            for g in (f, demes + f):
                centers = [potential[g, t, r, :] for t in range(spans)]
                steps = [centers[t] - potential[g, t, below, :] for t in range(spans - 1)]
                if k:
                    easts = shifted_east(centers, lane)
                    steps += [centers[t] - easts[t] for t in range(spans)]
                differ.append(steps)
            products = [a * b for a, b in zip(*differ)]
            for t in range(spans - 1):
                down[t] = products[t] if f == 0 else down[t] + products[t]
            for t in range(spans if k else 0):
                value = products[spans - 1 + t]
                right[t] = value if f == 0 else right[t] + value
        centers = [scaled[t, r, :] for t in range(spans)]
        for t in range(spans - 1):
            linked = jnp.minimum(centers[t], scaled[t, below, :]) > 0.0
            across[t, r, :] = jnp.where(linked, down[t], 0.0)
        if k:
            easts = shifted_east(centers, lane)
            right = [
                jnp.where(jnp.minimum(centers[t], easts[t]) > 0.0, right[t], 0.0) for t in range(spans)
            ]
            turned = [pltpu.roll(v, 1, 1) for v in right]
            above = slice(k * SUBS - 1, (k + 1) * SUBS - 1)
            for t in range(spans - 1):
                left = jnp.where(lane == 0, turned[t - 1], turned[t])
                value = (across[t, r, :] + across[t, above, :]) + (right[t] + left)
                grad[(k - 1) * SUBS : k * SUBS, t * LANES : (t + 1) * LANES] = -0.5 * value
    for flow in flows:
        flow.wait()


def on_device(sources, sample_maps, conductance, shunt, nodata_mask, deme_cells, pair_weights):
    demes, rows, cols = sources.shape
    fields = 2 * demes
    spans = cols // LANES + 1
    high = rows + 2 * SUBS
    slab = -(-((fields + 2) * ITERS + 1) // SUBS) * SUBS
    f32 = jnp.float32
    params = pltpu.CompilerParams(vmem_limit_bytes=LIMIT)
    block = [
        pltpu.with_memory_space_constraint(x, pltpu.HBM)
        for x in (sources, sample_maps, conductance, shunt, nodata_mask, deme_cells, pair_weights)
    ]
    count_r, count_c = lax.axis_size("rows"), lax.axis_size("cols")

    raw, send_c, send_d = pl.pallas_call(
        first_and_cols,
        out_shape=[pltpu.VMEM((fields + 2, spans, high, LANES), f32)]
        + [jax.ShapeDtypeStruct((rows, LANES), f32)] * 2,
        in_specs=[pl.BlockSpec(memory_space=pltpu.HBM)] * 7,
        out_specs=[VMEM] * 3,
        scratch_shapes=[
            pltpu.SMEM(deme_cells.shape, jnp.int32),
            pltpu.SMEM(pair_weights.shape, f32),
            pltpu.VMEM((rows, cols), f32),
            pltpu.VMEM((rows, cols), jnp.int32),
            pltpu.SemaphoreType.DMA((4 + 3 * (spans - 1),)),
        ],
        compiler_params=params,
        name="first_and_cols",
    )(*block)
    got_d = lax.ppermute(send_d, "cols", swaps(count_c, 1))
    got_c = lax.ppermute(send_c, "cols", swaps(count_c, 0))
    send_a, send_b = pl.pallas_call(
        pack_rows,
        out_shape=[jax.ShapeDtypeStruct((slab + SUBS, cols), f32)] * 2,
        in_specs=[VMEM] * 3,
        out_specs=[VMEM] * 2,
        compiler_params=params,
        name="pack_rows",
    )(raw, got_d, got_c)
    got_b = lax.ppermute(send_b, "rows", swaps(count_r, 1))
    got_a = lax.ppermute(send_a, "rows", swaps(count_r, 0))

    everyone = count_r * count_c
    basis_shape = pltpu.VMEM((ITERS, fields, spans, high, LANES), f32)
    sums_shape = pltpu.VMEM((2 * ITERS, fields, SUBS, LANES), f32)
    plane = pltpu.VMEM((spans, high, LANES), f32)
    flat = [pltpu.VMEM((4, spans, high, LANES), f32)] + [plane] * 3
    basis, sums = pl.pallas_call(
        inner_rows,
        out_shape=[basis_shape, sums_shape],
        in_specs=[VMEM] * 3,
        out_specs=[VMEM] * 2,
        scratch_shapes=[plane] + flat,
        compiler_params=params,
        cost_estimate=pl.CostEstimate(flops=40_000_000, bytes_accessed=20_000_000, transcendentals=0),
        name="inner_rows",
    )(raw, got_d, got_c)
    basis, _, scaled, message = pl.pallas_call(
        outer_rows,
        out_shape=[basis_shape, sums_shape, plane, jax.ShapeDtypeStruct((everyone, SUBS // 2, LANES), f32)],
        in_specs=[VMEM] * 7,
        out_specs=[VMEM] * 4,
        scratch_shapes=flat + [pltpu.VMEM((fields, spans, SUBS, LANES), f32)],
        input_output_aliases={5: 0, 6: 1},
        compiler_params=params,
        name="outer_rows",
    )(raw, got_d, got_c, got_b, got_a, basis, sums)
    gathered = lax.all_to_all(message, ("rows", "cols"), 0, 0)
    return pl.pallas_call(
        combine,
        out_shape=[
            jax.ShapeDtypeStruct((fields, rows, cols), f32),
            jax.ShapeDtypeStruct((rows, cols), f32),
        ],
        in_specs=[VMEM] * 3,
        out_specs=[pl.BlockSpec(memory_space=pltpu.HBM), VMEM],
        scratch_shapes=[
            pltpu.VMEM((fields, spans, high, LANES), f32),
            plane,
            pltpu.SemaphoreType.DMA((fields // 4 * (spans - 1),)),
        ],
        compiler_params=params,
        name="combine",
    )(gathered, basis, scaled)


def solution(mesh):
    return jax.shard_map(
        on_device,
        mesh=mesh,
        in_specs=(
            P(None, "rows", "cols"),
            P(None, "rows", "cols"),
            P("rows", "cols"),
            P("rows", "cols"),
            P("rows", "cols"),
            P(),
            P(),
        ),
        out_specs=(P(None, "rows", "cols"), P("rows", "cols")),
        check_vma=False,
    )
```
